256 devices in a mesh: dp: 4 (over y), tm: 16 (over z, core), rows: 4 (over x).
Axes of the slice: x: 4, y: 4, z: 8, core: 2. Of those that a mesh axis runs over, the one named last changes fastest.
Arguments:
- latents: bfloat16 [8, 32, 8, 192, 128], P('dp', 'tm', 'rows'), may hold values from -6 to 6
- slot_tile: int32 [4], replicated, may hold values from 0 to 7, as said below
- norm_gain: float32 [192], replicated, may hold values from 0.1 to 1.9
- conv_weight: bfloat16 [3, 3, 3, 192, 192], replicated, may hold values from -0.078125 to 0.078125
- up_weight: bfloat16 [3, 3, 96, 192], replicated, may hold values from -0.15625 to 0.15625
Outputs:
- pixels: bfloat16 [8, 32, 16, 96, 256], P('dp', 'tm', 'rows')
The draws below stay inside these ranges and needn't reach their ends.
Inputs may be any that keep to these rules, and one draw needn't show every extreme that they name: `slot_tile`: the values are distinct tile indices; tile 0 and tile 8 - 1 are always among them.
All inputs are finite; a program needn't handle non-finite values.
Results may differ from the reference program's by a relative error of at most 0.0052.
Values may be sent and summed in bfloat16 or wider, within the bound.
No kernel may reach another device: no remote copies, remote signals or barrier semaphores. Data moves between devices by JAX's collectives and lax.ppermute only.
A program may use at most 128 MiB of HBM per device.

```python
import jax
import jax.numpy as jnp
from jax import lax

C = 192
C2 = 96
W = 128
WORK = 1
TILES = 8
NF = 32
NR = 8
N_DP = 4


def draw_slot_tile(key, part):
    key = jax.random.fold_in(key, 7)
    first_key, second_key = jax.random.split(key)
    count = N_DP * WORK
    inner = jax.random.permutation(first_key, TILES - 2)[:count - 2] + 1
    picked = jnp.concatenate([jnp.array([0, TILES - 1], jnp.int32), inner.astype(jnp.int32)])
    order = jax.random.permutation(second_key, count)
    return picked[order].astype(jnp.int32)


def levels(stream_key, shape, shards, low, largest):
    level = 1.0
    for position, blocks in shards:
        draws = jax.random.uniform(jax.random.fold_in(jax.random.fold_in(stream_key, 6), position), (blocks,), jnp.float32, low / len(shards), largest / len(shards))
        level = level * jnp.repeat(jnp.exp(draws), shape[position] // blocks).reshape((-1,) + (1,) * (len(shape) - 1 - position))
    return level


def centred(own_key, extent, scale, bound, cuts=(), held_as=jnp.bfloat16):
    values = scale * jax.random.normal(own_key, extent, jnp.float32)
    if cuts:
        values = values * levels(own_key, extent, cuts, -0.22, 0.18)
    return jnp.clip(values, -bound, bound).astype(held_as)


def setup_inputs(seed: int = 0) -> dict:
    streams_of = jax.random.split(jax.random.key(seed), 6)
    latents = centred(streams_of[0], (TILES, NF, NR, C, W), 1.0, 6.0, ((0, 4), (1, 16), (2, 4)))
    slot_tile = draw_slot_tile(jax.random.fold_in(streams_of[5], 71), 0)
    norm_gain = jnp.clip(1.0 + 0.18 * jax.random.normal(streams_of[2], (C,), jnp.float32), 0.1, 1.9)
    conv_weight = centred(streams_of[3], (3, 3, 3, C, C), (27 * C) ** -0.5, 0.078125)
    up_weight = centred(streams_of[4], (3, 3, C2, C), (9 * C) ** -0.5, 0.15625)
    return {"latents": latents, "slot_tile": slot_tile, "norm_gain": norm_gain, "conv_weight": conv_weight, "up_weight": up_weight}


def activate(features, norm_gain):
    values = features.astype(jnp.float32)
    meansq = lax.optimization_barrier(jnp.mean(values * values, axis=-2, keepdims=True))
    normed = values * lax.rsqrt(meansq + 1e-06) * norm_gain.astype(jnp.float32)[:, None]
    return jax.nn.silu(normed).astype(jnp.bfloat16)

def decode_tile(tile, norm_gain, conv_weight, up_weight):
    frames, height, chans, cols = tile.shape
    padded = jnp.pad(tile, ((2, 0), (1, 1), (0, 0), (1, 1)))
    activated = activate(padded, norm_gain).astype(jnp.float32)
    weights = conv_weight.astype(jnp.float32)
    total = jnp.zeros((frames, height, conv_weight.shape[3], cols), jnp.float32)
    for tap_time in range(3):
        for tap_row in range(3):
            for tap_col in range(3):
                window = activated[tap_time:tap_time + frames, tap_row:tap_row + height, :, tap_col:tap_col + cols]
                total = total + jnp.einsum('frcw,oc->frow', window, weights[tap_time, tap_row, tap_col])
    hidden = (tile.astype(jnp.float32) + total).astype(jnp.bfloat16)
    upsampled = jnp.repeat(jnp.repeat(hidden, 2, axis=1), 2, axis=3)
    upsampled = jnp.pad(upsampled, ((0, 0), (1, 1), (0, 0), (1, 1))).astype(jnp.float32)
    up_float = up_weight.astype(jnp.float32)
    result = jnp.zeros((frames, 2 * height, up_weight.shape[2], 2 * cols), jnp.float32)
    for tap_row in range(3):
        for tap_col in range(3):
            window = upsampled[:, tap_row:tap_row + 2 * height, :, tap_col:tap_col + 2 * cols]
            result = result + jnp.einsum('frcw,oc->frow', window, up_float[tap_row, tap_col])
    return result.astype(jnp.bfloat16)

def reference(latents, slot_tile, norm_gain, conv_weight, up_weight):

    def one_slot(index):
        tile = lax.dynamic_index_in_dim(latents, index, 0, keepdims=False)
        return decode_tile(tile, norm_gain, conv_weight, up_weight)
    decoded = lax.map(one_slot, slot_tile)
    shape = (latents.shape[0],) + decoded.shape[1:]
    return jnp.zeros(shape, jnp.bfloat16).at[slot_tile].set(decoded)
```

```python
import functools

import jax
import jax.numpy as jnp
from jax import lax
from jax.experimental import pallas as pl
from jax.experimental.pallas import tpu as pltpu
from jax.sharding import PartitionSpec as P

C = 192
C2 = 96
W = 128
VMEM_LIMIT = 24 * 1024 * 1024


def activate(x, gain):
    meansq = jnp.mean(x * x, axis=0, keepdims=True)
    g = x * lax.rsqrt(meansq + 1e-06) * gain
    return (g * jax.nn.sigmoid(g)).astype(jnp.bfloat16)


def pair(ref, frame, row):
    return jnp.concatenate([ref[0, frame, row], ref[1, frame, row]], axis=1)


def shifted(p, by):
    lane = lax.broadcasted_iota(jnp.int32, (p.shape[0], W), 1)
    edge = 0 if by == 1 else W - 1
    halves = []
    for t in range(2):
        moved = pltpu.roll(p[:, t * W : (t + 1) * W], by % W, 1)
        halves.append(jnp.where(lane == edge, 0.0, moved))
    return jnp.concatenate(halves, axis=1)


def conv_terms(acts, w_ref, frame_out, row_out):
    acc = None
    for kt, panels in acts:
        for row in range(2):
            kh = row - row_out + 2
            if 0 <= kh <= 2:
                term = jnp.dot(w_ref[kt * 3 + kh], panels[row], preferred_element_type=jnp.float32)
                acc = term if acc is None else acc + term
    return shifted(acc[:C], 1) + acc[C : 2 * C] + shifted(acc[2 * C :], -1)


def own_kernel(x_ref, gain_ref, w_ref, s_ref):
    gain = gain_ref[...]
    xs = [[pair(x_ref, f, r).astype(jnp.float32) for r in range(2)] for f in range(2)]
    a = [[activate(xs[f][r], gain) for r in range(2)] for f in range(2)]
    for fo in range(2):
        for ro in range(4):
            acts = [(2 - (fo - fi), a[fi]) for fi in range(fo + 1)]
            total = conv_terms(acts, w_ref, fo, ro)
            if ro in (1, 2):
                total = total + xs[fo][ro - 1]
            s_ref[fo, ro] = total


def previous_kernel(x_ref, gain_ref, w_ref, s1_ref, s_ref, up_ref, down_ref):
    gain = gain_ref[...]
    a = [[activate(pair(x_ref, f, r).astype(jnp.float32), gain) for r in range(2)] for f in range(2)]
    for fo in range(2):
        for ro in range(4):
            acts = [(0, a[0]), (1, a[1])] if fo == 0 else [(0, a[1])]
            total = s1_ref[fo, ro] + conv_terms(acts, w_ref, fo, ro)
            s_ref[fo, ro] = total
            if ro < 2:
                up_ref[fo, ro] = total.astype(jnp.bfloat16)
            else:
                down_ref[fo, ro - 2] = total.astype(jnp.bfloat16)


def upsample_kernel(flag_ref, s_ref, above_ref, below_ref, w_ref, out_ref):
    keep = [flag_ref[0], flag_ref[1]]
    has = [flag_ref[2], flag_ref[3]]
    src = lax.broadcasted_iota(jnp.int32, (2 * W, 2 * W), 0)
    dst = lax.broadcasted_iota(jnp.int32, (2 * W, 2 * W), 1)
    spread = (dst == jnp.where(src < W, 2 * src, 2 * (src - W) + 1)).astype(jnp.bfloat16)
    for f in range(2):
        hidden = []
        for ro in range(4):
            there = has[0] if ro < 2 else has[1]
            got = (above_ref[f, ro] if ro < 2 else below_ref[f, ro - 2]).astype(jnp.float32)
            total = s_ref[f, ro] + got * there
            if ro in (0, 3):
                total = total * there
            hidden.append(total.astype(jnp.bfloat16))
        taps = {}
        for ro, khs in ((0, (0,)), (1, (0, 1, 2)), (2, (0, 1, 2)), (3, (2,))):
            for kh in khs:
                taps[kh, ro] = jnp.dot(w_ref[kh], hidden[ro], preferred_element_type=jnp.float32)
        for q in range(2):
            mid = taps[1, q + 1]
            for parity in range(2):
                if parity == 0:
                    rows = taps[0, q] + mid + taps[2, q + 1]
                else:
                    rows = taps[0, q + 1] + mid + taps[2, q + 2]
                k0, k1, k2 = rows[:C2], rows[C2 : 2 * C2], rows[2 * C2 :]
                even = (shifted(k0, 1) + k1 + k2).astype(jnp.bfloat16)
                odd = (k0 + k1 + shifted(k2, -1)).astype(jnp.bfloat16)
                for t in range(2):
                    both = jnp.concatenate([even[:, t * W : (t + 1) * W], odd[:, t * W : (t + 1) * W]], axis=1)
                    wide = jnp.dot(both, spread, preferred_element_type=jnp.float32)
                    out_ref[t, f, 2 * q + parity] = (wide * keep[t]).astype(jnp.bfloat16)


def call(kernel, out_shape, n_in, flops, smem_first=False):
    specs = [pl.BlockSpec(memory_space=pltpu.VMEM)] * n_in
    if smem_first:
        specs[0] = pl.BlockSpec(memory_space=pltpu.SMEM)
    several = isinstance(out_shape, tuple)
    vmem = pl.BlockSpec(memory_space=pltpu.VMEM)
    return pl.pallas_call(
        kernel,
        out_shape=out_shape,
        in_specs=specs,
        out_specs=(vmem,) * len(out_shape) if several else vmem,
        compiler_params=pltpu.CompilerParams(vmem_limit_bytes=VMEM_LIMIT),
        cost_estimate=pl.CostEstimate(flops=flops, bytes_accessed=4_000_000, transcendentals=0),
    )


def on_device(latents, slot_tile, norm_gain, conv_weight, up_weight):
    own_tiles, frames, rows = latents.shape[:3]
    tiles = lax.axis_index("dp") * own_tiles + jnp.arange(own_tiles, dtype=jnp.int32)
    keep = jnp.any(slot_tile[None, :] == tiles[:, None], axis=1).astype(jnp.float32)
    count = lax.axis_size("rows")
    me = lax.axis_index("rows")
    has = jnp.stack([me > 0, me < count - 1]).astype(jnp.float32)
    flags = jnp.concatenate([keep, has])
    gain = norm_gain[:, None]
    w = conv_weight.reshape(9, 3 * C, C)
    uw = up_weight.reshape(3, 3 * C2, C)

    steps = lax.axis_size("tm")
    previous = lax.ppermute(latents, "tm", [(i, i + 1) for i in range(steps - 1)])
    f32 = jnp.float32
    part = jax.ShapeDtypeStruct((2, 4, C, 2 * W), f32)
    half = jax.ShapeDtypeStruct((2, 2, C, 2 * W), jnp.bfloat16)
    s1 = call(own_kernel, part, 3, 1_020_000_000)(latents, gain, w)
    s, up, down = call(previous_kernel, (part, half, half), 4, 1_020_000_000)(previous, gain, w, s1)
    ring = [(i, (i + 1) % count) for i in range(count)]
    above = lax.ppermute(down, "rows", ring)
    below = lax.ppermute(up, "rows", [(j, i) for i, j in ring])
    out = jax.ShapeDtypeStruct((own_tiles, frames, 2 * rows, C2, 2 * W), jnp.bfloat16)
    return call(upsample_kernel, out, 5, 900_000_000, True)(flags, s, above, below, uw)


def solution(mesh):
    placed = (P("dp", "tm", "rows", None, None), P(), P(), P(), P())
    return jax.shard_map(
        on_device,
        mesh=mesh,
        in_specs=placed,
        out_specs=P("dp", "tm", "rows", None, None),
        check_vma=False,
    )
```

```python
import functools

import jax
import jax.numpy as jnp
from jax import lax
from jax.experimental import pallas as pl
from jax.experimental.pallas import tpu as pltpu
from jax.sharding import PartitionSpec as P

C = 192
C2 = 96
W = 128
VMEM_LIMIT = 16 * 1024 * 1024
AXES = ("dp", "tm", "rows")


def activate(x, gain):
    meansq = jnp.mean(x * x, axis=0, keepdims=True)
    g = x * lax.rsqrt(meansq + 1e-06) * gain
    return (g * jax.nn.sigmoid(g)).astype(jnp.bfloat16)


def column(row):
    i = lax.broadcasted_iota(jnp.int32, (C, C), 0)
    j = lax.broadcasted_iota(jnp.int32, (C, C), 1)
    return jnp.sum(jnp.where(i == j, row, 0.0), axis=1, keepdims=True)


def pair(ref, frame, row):
    return jnp.concatenate([ref[0, frame, row], ref[1, frame, row]], axis=1)


def shifted(p, by):
    lane = lax.broadcasted_iota(jnp.int32, (p.shape[0], W), 1)
    edge = 0 if by == 1 else W - 1
    halves = []
    for t in range(2):
        moved = pltpu.roll(p[:, t * W : (t + 1) * W], by % W, 1)
        halves.append(jnp.where(lane == edge, 0.0, moved))
    return jnp.concatenate(halves, axis=1)


def conv_terms(acts, w_ref, row_out):
    acc = None
    for kt, panels in acts:
        for row in range(2):
            kh = row - row_out + 2
            if 0 <= kh <= 2:
                term = jnp.dot(w_ref[kt * 3 + kh], panels[row], preferred_element_type=jnp.float32)
                acc = term if acc is None else acc + term
    return shifted(acc[:C], 1) + acc[C : 2 * C] + shifted(acc[2 * C :], -1)


def own_kernel(x_hbm, gain_hbm, w_hbm, uw_hbm, s_ref, w_ref, uw_ref, gain_ref, x_ref, sem, w_sem):
    copies = [
        pltpu.make_async_copy(x_hbm, x_ref, sem.at[0]),
        pltpu.make_async_copy(gain_hbm, gain_ref, sem.at[1]),
    ]
    order = [6, 7, 8, 3, 4, 5, 0, 1, 2]
    weights = {k: pltpu.make_async_copy(w_hbm.at[k], w_ref.at[k], w_sem.at[k]) for k in order}
    last = pltpu.make_async_copy(uw_hbm, uw_ref, sem.at[2])
    for copy in copies + [weights[k] for k in order] + [last]:
        copy.start()
    for copy in copies:
        copy.wait()
    gain = column(gain_ref[...])
    xs = [[pair(x_ref, f, r).astype(jnp.float32) for r in range(2)] for f in range(2)]
    a = [[activate(xs[f][r], gain) for r in range(2)] for f in range(2)]
    for k in order:
        weights[k].wait()
    for fo in range(2):
        for ro in range(4):
            total = conv_terms([(2 - (fo - fi), a[fi]) for fi in range(fo + 1)], w_ref, ro)
            if ro in (1, 2):
                total = total + xs[fo][ro - 1]
            s_ref[fo, ro] = total
    last.wait()


def previous_kernel(core, at_ref, x_ref, gain_ref, w_ref, s1_ref, *refs):
    s_ref, first_ref, second_ref = refs[-3:]
    tm, row = at_ref[1], at_ref[2]

    @pl.when(lax.rem(tm, 2) == core)
    def _():
        gain = column(gain_ref[...])
        a = [[activate(pair(x_ref, f, r).astype(jnp.float32), gain) for r in range(2)] for f in range(2)]
        a = [[jnp.where(tm > 0, p, jnp.zeros_like(p)) for p in ps] for ps in a]
        upper = lax.rem(row, 2) == 0
        for fo in range(2):
            acts = [(0, a[0]), (1, a[1])] if fo == 0 else [(0, a[1])]
            for k in range(2):
                sent = []
                for ro in (k, k + 2):
                    total = s1_ref[fo, ro] + conv_terms(acts, w_ref, ro)
                    s_ref[fo, ro] = total
                    sent.append(total.astype(jnp.bfloat16))
                first_ref[fo, k] = jnp.where(upper, sent[1], sent[0])
                second_ref[fo, k] = jnp.where(upper, sent[0], sent[1])


def upsample_kernel(core, rows, at_ref, slot_ref, s_ref, first_ref, second_ref, w_ref, *refs):
    out_ref, buf_ref, sem = refs[-3:]
    dp, tm, row = at_ref[0], at_ref[1], at_ref[2]

    @pl.when(lax.rem(tm, 2) == core)
    def _():
        upper = lax.rem(row, 2) == 0
        keep = []
        for t in range(2):
            tile = dp * 2 + t
            hit = slot_ref[0] == tile
            for i in range(1, slot_ref.shape[0]):
                hit = jnp.logical_or(hit, slot_ref[i] == tile)
            keep.append(jnp.where(hit, 1.0, 0.0))
        above_there = jnp.where(row > 0, 1.0, 0.0)
        below_there = jnp.where(row < rows - 1, 1.0, 0.0)
        src = lax.broadcasted_iota(jnp.int32, (2 * W, 2 * W), 0)
        dst = lax.broadcasted_iota(jnp.int32, (2 * W, 2 * W), 1)
        spread = (dst == jnp.where(src < W, 2 * src, 2 * (src - W) + 1)).astype(jnp.bfloat16)
        copies = []
        for f in range(2):
            hidden = []
            for ro in range(4):
                there = above_there if ro < 2 else below_there
                ways = first_ref[f, ro % 2], second_ref[f, ro % 2]
                got = jnp.where(upper == (ro >= 2), *ways).astype(jnp.float32)
                if ro in (0, 3):
                    total = (s_ref[f, ro] + got) * there
                else:
                    total = s_ref[f, ro] + got * there
                hidden.append(total.astype(jnp.bfloat16))
            taps = {}
            for ro, khs in ((0, (0,)), (1, (0, 1, 2)), (2, (0, 1, 2)), (3, (2,))):
                for kh in khs:
                    taps[kh, ro] = jnp.dot(w_ref[kh], hidden[ro], preferred_element_type=jnp.float32)
            for q in range(2):
                mid = taps[1, q + 1]
                for parity in range(2):
                    if parity == 0:
                        total = taps[0, q] + mid + taps[2, q + 1]
                    else:
                        total = taps[0, q + 1] + mid + taps[2, q + 2]
                    k0, k1, k2 = total[:C2], total[C2 : 2 * C2], total[2 * C2 :]
                    even = (shifted(k0, 1) + k1 + k2).astype(jnp.bfloat16)
                    odd = (k0 + k1 + shifted(k2, -1)).astype(jnp.bfloat16)
                    for t in range(2):
                        both = jnp.concatenate([even[:, t * W : (t + 1) * W], odd[:, t * W : (t + 1) * W]], axis=1)
                        wide = jnp.dot(both, spread, preferred_element_type=jnp.float32)
                        buf_ref[f, t, 2 * q + parity] = (wide * keep[t]).astype(jnp.bfloat16)
            for t in range(2):
                copy = pltpu.make_async_copy(buf_ref.at[f, t], out_ref.at[t, f], sem.at[f, t])
                copy.start()
                copies.append(copy)
        for copy in copies:
            copy.wait()


SMEM = pl.BlockSpec(memory_space=pltpu.SMEM)
VMEM = pl.BlockSpec(memory_space=pltpu.VMEM)
ANY = pl.BlockSpec(memory_space=pl.ANY)
HBM = pl.BlockSpec(memory_space=pltpu.HBM)


def call(kernel, out_shape, in_specs, flops, out_spec=VMEM, **more):
    out_specs = jax.tree.map(lambda _: out_spec, out_shape)
    return pl.pallas_call(
        kernel,
        out_shape=out_shape,
        in_specs=in_specs,
        out_specs=out_specs,
        compiler_params=pltpu.CompilerParams(vmem_limit_bytes=VMEM_LIMIT),
        cost_estimate=pl.CostEstimate(flops=flops, bytes_accessed=4_000_000, transcendentals=0),
        **more,
    )


def swap(value, partner):
    n_dp, n_tm, n_rows = (lax.axis_size(a) for a in AXES)

    def index(d, t, r):
        return (d * n_tm + t) * n_rows + r

    places = [(d, t, r) for d in range(n_dp) for t in range(n_tm) for r in range(n_rows)]
    return lax.ppermute(value, AXES, [(index(*p), index(*partner(*p))) for p in places])


def on_device(latents, slot_tile, norm_gain, conv_weight, up_weight):
    own_tiles, frames, rows = latents.shape[:3]
    n_dp, n_tm, n_rows = (lax.axis_size(a) for a in AXES)
    at = jnp.stack([lax.axis_index(a) for a in AXES]).astype(jnp.int32)
    gain = norm_gain.reshape(1, C)
    w = conv_weight.reshape(9, 3 * C, C)
    uw = up_weight.reshape(3, 3 * C2, C)

    def idle(phase):
        return lambda d: (d ^ 1) if phase == 0 else ((d + 1) % n_dp if d % 2 else (d - 1) % n_dp)

    def across_chips(d, t, r):
        if t in (0, n_tm - 1):
            return idle(0)(d), t, r
        return d, (t + 1 if t % 2 else t - 1), r

    def rows_swap(phase, core):
        def partner(d, t, r):
            if t % 2 != core:
                return idle(phase)(d), t, r
            if phase == 0:
                return d, t, r ^ 1
            return d, t, ((r + 1) % n_rows if r % 2 else (r - 1) % n_rows)

        return partner

    part = jax.ShapeDtypeStruct((2, 4, C, 2 * W), jnp.float32)
    half = jax.ShapeDtypeStruct((2, 2, C, 2 * W), jnp.bfloat16)

    from_chip = swap(latents, lambda d, t, r: (d, t ^ 1, r))
    from_z = swap(latents, across_chips)
    s1, w, uw, gain = call(
        own_kernel,
        (part, *(jax.ShapeDtypeStruct(v.shape, v.dtype) for v in (w, uw, gain))),
        [HBM] * 4,
        1_020_000_000,
        scratch_shapes=[
            pltpu.VMEM(latents.shape, latents.dtype),
            pltpu.SemaphoreType.DMA((3,)),
            pltpu.SemaphoreType.DMA((9,)),
        ],
    )(*(pltpu.with_memory_space_constraint(v, pltpu.HBM) for v in (latents, gain, w, uw)))
    specs = [SMEM] + [VMEM] * 4
    s, odd1, odd2 = call(
        functools.partial(previous_kernel, 1), (part, half, half), specs, 1_020_000_000
    )(at, from_chip, gain, w, s1)
    odd1 = swap(odd1, rows_swap(0, 1))
    odd2 = swap(odd2, rows_swap(1, 1))
    s, even1, even2 = call(
        functools.partial(previous_kernel, 0),
        (part, half, half),
        specs + [VMEM],
        1_020_000_000,
        input_output_aliases={5: 0},
    )(at, from_z, gain, w, s1, s)
    even1 = swap(even1, rows_swap(0, 0))
    even2 = swap(even2, rows_swap(1, 0))
    out = jax.ShapeDtypeStruct((own_tiles, frames, 2 * rows, C2, 2 * W), jnp.bfloat16)
    scratch = [pltpu.VMEM((2, 2, 2 * rows, C2, 2 * W), jnp.bfloat16), pltpu.SemaphoreType.DMA((2, 2))]
    specs = [SMEM, SMEM] + [VMEM] * 4
    pixels = call(
        functools.partial(upsample_kernel, 1, n_rows), out, specs, 9_000_000_000, ANY, scratch_shapes=scratch
    )(at, slot_tile, s, odd1, odd2, uw)
    return call(
        functools.partial(upsample_kernel, 0, n_rows),
        out,
        specs + [ANY],
        900_000_000,
        ANY,
        scratch_shapes=scratch,
        input_output_aliases={6: 0},
    )(at, slot_tile, s, even1, even2, uw, pixels)


def solution(mesh):
    placed = (P("dp", "tm", "rows", None, None), P(), P(), P(), P())
    return jax.shard_map(
        on_device,
        mesh=mesh,
        in_specs=placed,
        out_specs=P("dp", "tm", "rows", None, None),
        check_vma=False,
    )
```

```python
import functools

import jax
import jax.numpy as jnp
from jax import lax
from jax.experimental import pallas as pl
from jax.experimental.pallas import tpu as pltpu
from jax.sharding import PartitionSpec as P

C = 192
C2 = 96
W = 128
VMEM_LIMIT = 16 * 1024 * 1024
AXES = ("dp", "tm", "rows")


def activate(x, gain):
    meansq = jnp.mean(x * x, axis=0, keepdims=True)
    g = x * lax.rsqrt(meansq + 1e-06) * gain
    return (g * jax.nn.sigmoid(g)).astype(jnp.bfloat16)


def column(row):
    i = lax.broadcasted_iota(jnp.int32, (C, C), 0)
    j = lax.broadcasted_iota(jnp.int32, (C, C), 1)
    return jnp.sum(jnp.where(i == j, row, 0.0), axis=1, keepdims=True)


def pair(ref, frame, row):
    return jnp.concatenate([ref[0, frame, row], ref[1, frame, row]], axis=1)


def shifted(p, by):
    lane = lax.broadcasted_iota(jnp.int32, (p.shape[0], W), 1)
    edge = 0 if by == 1 else W - 1
    halves = []
    for t in range(2):
        moved = pltpu.roll(p[:, t * W : (t + 1) * W], by % W, 1)
        halves.append(jnp.where(lane == edge, 0.0, moved))
    return jnp.concatenate(halves, axis=1)


def conv_terms(acts, w_ref, row_out, flip):
    acc = None
    for kt, panels in acts:
        for row in range(2):
            kh = row - row_out + 2
            if 0 <= kh <= 2:
                tap = kt * 3 + jnp.where(flip, 2 - kh, kh)
                term = jnp.dot(w_ref[tap], panels[row], preferred_element_type=jnp.float32)
                acc = term if acc is None else acc + term
    return shifted(acc[:C], 1) + acc[C : 2 * C] + shifted(acc[2 * C :], -1)


def flipped():
    return lax.rem(lax.axis_index("rows"), 2) == 1


def panels(x_ref, flip):
    rows = [jnp.where(flip, 1 - r, r) for r in range(2)]
    return [[pair(x_ref, f, r).astype(jnp.float32) for r in rows] for f in range(2)]


def own_kernel(x_hbm, gain_hbm, w_hbm, uw_hbm, s_ref, w_ref, uw_ref, gain_ref, x_ref, sem, w_sem):
    copies = [
        pltpu.make_async_copy(x_hbm, x_ref, sem.at[0]),
        pltpu.make_async_copy(gain_hbm, gain_ref, sem.at[1]),
    ]
    order = [6, 7, 8, 3, 4, 5, 0, 1, 2]
    weights = {k: pltpu.make_async_copy(w_hbm.at[k], w_ref.at[k], w_sem.at[k]) for k in order}
    last = pltpu.make_async_copy(uw_hbm, uw_ref, sem.at[2])
    for copy in copies + [weights[k] for k in order] + [last]:
        copy.start()
    for copy in copies:
        copy.wait()
    flip = flipped()
    gain = column(gain_ref[...])
    xs = panels(x_ref, flip)
    a = [[activate(xs[f][r], gain) for r in range(2)] for f in range(2)]
    for fo in range(2):
        for k in ((6, 7, 8), (3, 4, 5))[fo]:
            weights[k].wait()
        for ro in range(4):
            total = conv_terms([(2 - (fo - fi), a[fi]) for fi in range(fo + 1)], w_ref, ro, flip)
            if ro in (1, 2):
                total = total + xs[fo][ro - 1]
            s_ref[fo, ro] = total
    for k in (0, 1, 2):
        weights[k].wait()
    last.wait()


def previous_kernel(core, x_ref, gain_ref, w_ref, s1_ref, uw_ref, *refs):
    s_ref, first_ref, second_ref, u_ref = refs[-4:]
    tm = lax.axis_index("tm")
    flip = flipped()

    @pl.when(lax.rem(tm, 2) == core)
    def _():
        gain = jnp.where(tm > 0, column(gain_ref[...]), 0.0)
        a = [[activate(x, gain) for x in xs] for xs in panels(x_ref, flip)]
        for fo in range(2):
            acts = [(0, a[0]), (1, a[1])] if fo == 0 else [(0, a[1])]
            for ro in range(4):
                total = s1_ref[fo, ro] + conv_terms(acts, w_ref, ro, flip)
                s_ref[fo, ro] = total
                to_ref = first_ref if ro >= 2 else second_ref
                to_ref[fo, ro % 2] = total.astype(jnp.bfloat16)

    @pl.when(lax.rem(tm, 2) != core)
    def _():
        w0, w1, w2 = (uw_ref[jnp.where(flip, 2 - kh, kh)].astype(jnp.float32) for kh in range(3))
        u_ref[0] = jnp.concatenate([w0, w1 + w2], axis=1).astype(jnp.bfloat16)
        u_ref[1] = jnp.concatenate([w0 + w1, w2], axis=1).astype(jnp.bfloat16)


def upsample_kernel(core, s_ref, first_ref, second_ref, u_ref, slot_ref, *refs):
    out_ref, h_ref, b_ref, buf_ref, sem = refs[-5:]
    row, rows = lax.axis_index("rows"), lax.axis_size("rows")

    @pl.when(lax.rem(lax.axis_index("tm"), 2) == core)
    def _():
        flip = flipped()
        src = lax.broadcasted_iota(jnp.int32, (2 * W, 2 * W), 0)
        dst = lax.broadcasted_iota(jnp.int32, (2 * W, 2 * W), 1)
        spread = (dst == jnp.where(src < W, 2 * src, 2 * (src - W) + 1)).astype(jnp.bfloat16)
        keep = []
        for t in range(2):
            hit = slot_ref[...] == lax.axis_index("dp") * 2 + t
            keep.append(jnp.max(jnp.where(hit, 1.0, 0.0), axis=1, keepdims=True))
        inside = jnp.where(jnp.logical_and(row > 0, row < rows - 1), 1.0, 0.0)
        copies = []
        for f in range(2):
            for ro in range(4):
                got = (first_ref if ro >= 2 else second_ref)[f, 1 - ro % 2].astype(jnp.float32)
                total = s_ref[f, ro]
                if ro == 0:
                    total = (total + got) * inside
                elif ro == 1:
                    total = total + got * inside
                else:
                    total = total + got
                h_ref[f, ro * C : (ro + 1) * C] = total.astype(jnp.bfloat16)
            for q in range(2):
                for parity in range(2):
                    low = (q + parity) * C
                    total = jnp.dot(u_ref[parity], h_ref[f, low : low + 2 * C], preferred_element_type=jnp.float32)
                    k0, k1, k2 = total[:C2], total[C2 : 2 * C2], total[2 * C2 :]
                    even = (shifted(k0, 1) + k1 + k2).astype(jnp.bfloat16)
                    odd = (k0 + k1 + shifted(k2, -1)).astype(jnp.bfloat16)
                    for t in range(2):
                        at = (t * 4 + 2 * q + parity) * C2
                        b_ref[f, at : at + C2, :W] = even[:, t * W : (t + 1) * W]
                        b_ref[f, at : at + C2, W:] = odd[:, t * W : (t + 1) * W]
            for t in range(2):
                wide = jnp.dot(b_ref[f, t * 4 * C2 : (t + 1) * 4 * C2], spread, preferred_element_type=jnp.float32)
                wide = (wide * keep[t]).astype(jnp.bfloat16)
                for at_row in range(4):
                    to_row = jnp.where(flip, 3 - at_row, at_row)
                    buf_ref[f, t, to_row] = wide[at_row * C2 : (at_row + 1) * C2]
                copy = pltpu.make_async_copy(buf_ref.at[f, t], out_ref.at[t, f], sem.at[f, t])
                copy.start()
                copies.append(copy)
        for copy in copies:
            copy.wait()


VMEM = pl.BlockSpec(memory_space=pltpu.VMEM)
ANY = pl.BlockSpec(memory_space=pl.ANY)
HBM = pl.BlockSpec(memory_space=pltpu.HBM)


def call(kernel, out_shape, in_specs, flops, out_spec=VMEM, **more):
    out_specs = jax.tree.map(lambda _: out_spec, out_shape)
    return pl.pallas_call(
        kernel,
        out_shape=out_shape,
        in_specs=in_specs,
        out_specs=out_specs,
        compiler_params=pltpu.CompilerParams(vmem_limit_bytes=VMEM_LIMIT),
        cost_estimate=pl.CostEstimate(flops=flops, bytes_accessed=4_000_000, transcendentals=0),
        **more,
    )


def swap(value, partner):
    n_dp, n_tm, n_rows = (lax.axis_size(a) for a in AXES)

    def index(d, t, r):
        return (d * n_tm + t) * n_rows + r

    places = [(d, t, r) for d in range(n_dp) for t in range(n_tm) for r in range(n_rows)]
    return lax.ppermute(value, AXES, [(index(*p), index(*partner(*p))) for p in places])


def on_device(latents, slot_tile, norm_gain, conv_weight, up_weight):
    own_tiles, frames, rows = latents.shape[:3]
    n_dp, n_tm, n_rows = (lax.axis_size(a) for a in AXES)
    slots = slot_tile.reshape(1, -1)
    gain = norm_gain.reshape(1, C)
    w = conv_weight.reshape(9, 3 * C, C)
    uw = up_weight.reshape(3, 3 * C2, C)

    def idle(phase):
        return lambda d: (d ^ 1) if phase == 0 else ((d + 1) % n_dp if d % 2 else (d - 1) % n_dp)

    def across_chips(d, t, r):
        if t in (0, n_tm - 1):
            return idle(0)(d), t, r
        return d, (t + 1 if t % 2 else t - 1), r

    def rows_swap(phase, core):
        def partner(d, t, r):
            if t % 2 != core:
                return idle(phase)(d), t, r
            if phase == 0:
                return d, t, r ^ 1
            return d, t, ((r + 1) % n_rows if r % 2 else (r - 1) % n_rows)

        return partner

    part = jax.ShapeDtypeStruct((2, 4, C, 2 * W), jnp.float32)
    half = jax.ShapeDtypeStruct((2, 2, C, 2 * W), jnp.bfloat16)

    from_chip = swap(latents, lambda d, t, r: (d, t ^ 1, r))
    from_z = swap(latents, across_chips)
    s1, w, uw, gain = call(
        own_kernel,
        (part, *(jax.ShapeDtypeStruct(v.shape, v.dtype) for v in (w, uw, gain))),
        [HBM] * 4,
        1_020_000_000,
        scratch_shapes=[
            pltpu.VMEM(latents.shape, latents.dtype),
            pltpu.SemaphoreType.DMA((3,)),
            pltpu.SemaphoreType.DMA((9,)),
        ],
    )(*(pltpu.with_memory_space_constraint(v, pltpu.HBM) for v in (latents, gain, w, uw)))
    specs = [VMEM] * 5
    wide = jax.ShapeDtypeStruct((2, 3 * C2, 2 * C), jnp.bfloat16)
    s, odd1, odd2, u = call(
        functools.partial(previous_kernel, 1), (part, half, half, wide), specs, 1_020_000_000
    )(from_chip, gain, w, s1, uw)
    odd1 = swap(odd1, rows_swap(0, 1))
    odd2 = swap(odd2, rows_swap(1, 1))
    s, even1, even2, u = call(
        functools.partial(previous_kernel, 0),
        (part, half, half, wide),
        specs + [VMEM] * 2,
        1_020_000_000,
        input_output_aliases={5: 0, 6: 3},
    )(from_z, gain, w, s1, uw, s, u)
    even1 = swap(even1, rows_swap(0, 0))
    even2 = swap(even2, rows_swap(1, 0))
    out = jax.ShapeDtypeStruct((own_tiles, frames, 2 * rows, C2, 2 * W), jnp.bfloat16)
    scratch = [
        pltpu.VMEM((2, 4 * C, 2 * W), jnp.bfloat16),
        pltpu.VMEM((2, 8 * C2, 2 * W), jnp.bfloat16),
        pltpu.VMEM((2, 2, 2 * rows, C2, 2 * W), jnp.bfloat16),
        pltpu.SemaphoreType.DMA((2, 2)),
    ]
    specs = [VMEM] * 5
    pixels = call(
        functools.partial(upsample_kernel, 1), out, specs, 9_000_000_000, ANY, scratch_shapes=scratch
    )(s, odd1, odd2, u, slots)
    return call(
        functools.partial(upsample_kernel, 0),
        out,
        specs + [ANY],
        900_000_000,
        ANY,
        scratch_shapes=scratch,
        input_output_aliases={5: 0},
    )(s, even1, even2, u, slots, pixels)


def solution(mesh):
    placed = (P("dp", "tm", "rows", None, None), P(), P(), P(), P())
    return jax.shard_map(
        on_device,
        mesh=mesh,
        in_specs=placed,
        out_specs=P("dp", "tm", "rows", None, None),
        check_vma=False,
    )
```

```python
import functools

import jax
import jax.numpy as jnp
from jax import lax
from jax.experimental import pallas as pl
from jax.experimental.pallas import tpu as pltpu
from jax.sharding import PartitionSpec as P

C = 192
C2 = 96
W = 128
VMEM_LIMIT = 16 * 1024 * 1024
AXES = ("dp", "tm", "rows")


def activate(x, gain):
    meansq = jnp.mean(x * x, axis=0, keepdims=True)
    g = x * lax.rsqrt(meansq + 1e-06) * gain
    return (g * jax.nn.sigmoid(g)).astype(jnp.bfloat16)


def column(row):
    i = lax.broadcasted_iota(jnp.int32, (C, C), 0)
    j = lax.broadcasted_iota(jnp.int32, (C, C), 1)
    return jnp.sum(jnp.where(i == j, row, 0.0), axis=1, keepdims=True)


def pair(ref, frame, row):
    return jnp.concatenate([ref[0, frame, row], ref[1, frame, row]], axis=1)


def shifted(p, by):
    lane = lax.broadcasted_iota(jnp.int32, (p.shape[0], W), 1)
    edge = 0 if by == 1 else W - 1
    halves = []
    for t in range(2):
        moved = pltpu.roll(p[:, t * W : (t + 1) * W], by % W, 1)
        halves.append(jnp.where(lane == edge, 0.0, moved))
    return jnp.concatenate(halves, axis=1)


def conv_terms(acts, w_ref, row_out, flip):
    acc = None
    for kt, panels in acts:
        for row in range(2):
            kh = row - row_out + 2
            if 0 <= kh <= 2:
                tap = kt * 3 + jnp.where(flip, 2 - kh, kh)
                term = jnp.dot(w_ref[tap], panels[row], preferred_element_type=jnp.float32)
                acc = term if acc is None else acc + term
    return shifted(acc[:C], 1) + acc[C : 2 * C] + shifted(acc[2 * C :], -1)


def flipped():
    return lax.rem(lax.axis_index("rows"), 2) == 1


def panels(x_ref, flip):
    rows = [jnp.where(flip, 1 - r, r) for r in range(2)]
    return [[pair(x_ref, f, r).astype(jnp.float32) for r in rows] for f in range(2)]


def spread_kernel(spread_ref):
    src = lax.broadcasted_iota(jnp.int32, (2 * W, 2 * W), 0)
    dst = lax.broadcasted_iota(jnp.int32, (2 * W, 2 * W), 1)
    spread_ref[...] = (dst == jnp.where(src < W, 2 * src, 2 * (src - W) + 1)).astype(jnp.bfloat16)


def own_kernel(x_ref, gain_ref, w_ref, spread_ref, s_ref, _):
    flip = flipped()
    gain = column(gain_ref[...])
    xs = panels(x_ref, flip)
    a = [[activate(xs[f][r], gain) for r in range(2)] for f in range(2)]
    for fo in range(2):
        for ro in range(4):
            total = conv_terms([(2 - (fo - fi), a[fi]) for fi in range(fo + 1)], w_ref, ro, flip)
            if ro in (1, 2):
                total = total + xs[fo][ro - 1]
            s_ref[fo, ro] = total


def previous_kernel(core, x_ref, gain_ref, w_ref, s1_ref, uw_ref, *refs):
    s_ref, first_ref, second_ref, u_ref = refs[-4:]
    tm = lax.axis_index("tm")
    flip = flipped()

    @pl.when(lax.rem(tm, 2) == core)
    def _():
        gain = jnp.where(tm > 0, column(gain_ref[...]), 0.0)
        a = [[activate(x, gain) for x in xs] for xs in panels(x_ref, flip)]
        for fo in range(2):
            acts = [(0, a[0]), (1, a[1])] if fo == 0 else [(0, a[1])]
            for ro in range(4):
                total = s1_ref[fo, ro] + conv_terms(acts, w_ref, ro, flip)
                s_ref[fo, ro] = total
                to_ref = first_ref if ro >= 2 else second_ref
                to_ref[fo, ro % 2] = total.astype(jnp.bfloat16)

    @pl.when(lax.rem(tm, 2) != core)
    def _():
        w0, w1, w2 = (uw_ref[jnp.where(flip, 2 - kh, kh)].astype(jnp.float32) for kh in range(3))
        u_ref[0] = jnp.concatenate([w0, w1 + w2], axis=1).astype(jnp.bfloat16)
        u_ref[1] = jnp.concatenate([w0 + w1, w2], axis=1).astype(jnp.bfloat16)


def upsample_kernel(core, edge, s_ref, u_ref, slot_ref, spread_ref, first_ref, *refs):
    out_ref, h_ref, b_ref, buf_ref, sem = refs[-5:]
    second_ref = refs[0]
    row, rows = lax.axis_index("rows"), lax.axis_size("rows")
    mine = lax.rem(lax.axis_index("tm"), 2) == core
    at_edge = jnp.logical_or(row == 0, row == rows - 1)

    if edge is not None:
        mine = jnp.logical_and(mine, at_edge == edge)

    @pl.when(mine)
    def _():
        flip = flipped()
        spread = spread_ref[...]
        keep = []
        for t in range(2):
            hit = slot_ref[...] == lax.axis_index("dp") * 2 + t
            keep.append(jnp.max(jnp.where(hit, 1.0, 0.0), axis=1, keepdims=True))
        copies = []
        for f in range(2):
            for ro in range(4):
                total = s_ref[f, ro]
                if ro >= 2 or not edge:
                    got = (first_ref if ro >= 2 else second_ref)[f, 1 - ro % 2]
                    total = total + got.astype(jnp.float32)
                if edge is None and ro < 2:
                    alone = s_ref[f, ro] if ro == 1 else jnp.zeros_like(total)
                    total = jnp.where(at_edge, alone, total)
                elif edge and ro == 0:
                    total = jnp.zeros_like(total)
                h_ref[f, ro * C : (ro + 1) * C] = total.astype(jnp.bfloat16)
            for q in range(2):
                for parity in range(2):
                    low = (q + parity) * C
                    total = jnp.dot(u_ref[parity], h_ref[f, low : low + 2 * C], preferred_element_type=jnp.float32)
                    k0, k1, k2 = total[:C2], total[C2 : 2 * C2], total[2 * C2 :]
                    even = (shifted(k0, 1) + k1 + k2).astype(jnp.bfloat16)
                    odd = (k0 + k1 + shifted(k2, -1)).astype(jnp.bfloat16)
                    for t in range(2):
                        at = (t * 4 + 2 * q + parity) * C2
                        b_ref[f, at : at + C2, :W] = even[:, t * W : (t + 1) * W]
                        b_ref[f, at : at + C2, W:] = odd[:, t * W : (t + 1) * W]
            for t in range(2):
                wide = jnp.dot(b_ref[f, t * 4 * C2 : (t + 1) * 4 * C2], spread, preferred_element_type=jnp.float32)
                wide = (wide * keep[t]).astype(jnp.bfloat16)
                for at_row in range(4):
                    to_row = jnp.where(flip, 3 - at_row, at_row)
                    buf_ref[f, t, to_row] = wide[at_row * C2 : (at_row + 1) * C2]
                copy = pltpu.make_async_copy(buf_ref.at[f, t], out_ref.at[t, f], sem.at[f, t])
                copy.start()
                copies.append(copy)
        for copy in copies:
            copy.wait()


VMEM = pl.BlockSpec(memory_space=pltpu.VMEM)
ANY = pl.BlockSpec(memory_space=pl.ANY)


def call(kernel, out_shape, in_specs, flops, out_spec=VMEM, **more):
    out_specs = jax.tree.map(lambda _: out_spec, out_shape)
    return pl.pallas_call(
        kernel,
        out_shape=out_shape,
        in_specs=in_specs,
        out_specs=out_specs,
        compiler_params=pltpu.CompilerParams(vmem_limit_bytes=VMEM_LIMIT),
        cost_estimate=pl.CostEstimate(flops=flops, bytes_accessed=4_000_000, transcendentals=0),
        **more,
    )


def swap(value, partner):
    n_dp, n_tm, n_rows = (lax.axis_size(a) for a in AXES)

    def index(d, t, r):
        return (d * n_tm + t) * n_rows + r

    places = [(d, t, r) for d in range(n_dp) for t in range(n_tm) for r in range(n_rows)]
    return lax.ppermute(value, AXES, [(index(*p), index(*partner(*p))) for p in places])


def on_device(latents, slot_tile, norm_gain, conv_weight, up_weight):
    own_tiles, frames, rows = latents.shape[:3]
    n_dp, n_tm, n_rows = (lax.axis_size(a) for a in AXES)
    slots = slot_tile.reshape(1, -1)
    gain = norm_gain.reshape(1, C)
    w = conv_weight.reshape(9, 3 * C, C)
    uw = up_weight.reshape(3, 3 * C2, C)

    def idle(phase):
        return lambda d: (d ^ 1) if phase == 0 else ((d + 1) % n_dp if d % 2 else (d - 1) % n_dp)

    def across_chips(d, t, r):
        if t in (0, n_tm - 1):
            return idle(0)(d), t, r
        return d, (t + 1 if t % 2 else t - 1), r

    def rows_swap(phase, core):
        def partner(d, t, r):
            if t % 2 != core:
                return idle(phase)(d), t, r
            if phase == 0:
                return d, t, r ^ 1
            return d, t, ((r + 1) % n_rows if r % 2 else (r - 1) % n_rows)

        return partner

    part = jax.ShapeDtypeStruct((2, 4, C, 2 * W), jnp.float32)
    half = jax.ShapeDtypeStruct((2, 2, C, 2 * W), jnp.bfloat16)

    from_chip = swap(latents, lambda d, t, r: (d, t ^ 1, r))
    from_z = swap(latents, across_chips)
    square = jax.ShapeDtypeStruct((2 * W, 2 * W), jnp.bfloat16)
    spread = call(spread_kernel, square, [], 9_000_000_000)()
    s1, spread = call(own_kernel, (part, square), [VMEM] * 4, 1_020_000_000, input_output_aliases={3: 1})(
        latents, gain, w, spread
    )
    specs = [VMEM] * 5
    wide = jax.ShapeDtypeStruct((2, 3 * C2, 2 * C), jnp.bfloat16)
    s, odd1, odd2, u = call(
        functools.partial(previous_kernel, 1), (part, half, half, wide), specs, 1_020_000_000
    )(from_chip, gain, w, s1, uw)
    odd1 = swap(odd1, rows_swap(0, 1))
    odd2 = swap(odd2, rows_swap(1, 1))
    s, even1, even2, u = call(
        functools.partial(previous_kernel, 0),
        (part, half, half, wide),
        specs + [VMEM] * 2,
        1_020_000_000,
        input_output_aliases={5: 0, 6: 3},
    )(from_z, gain, w, s1, uw, s, u)
    even1 = swap(even1, rows_swap(0, 0))
    even2 = swap(even2, rows_swap(1, 0))
    out = jax.ShapeDtypeStruct((own_tiles, frames, 2 * rows, C2, 2 * W), jnp.bfloat16)
    scratch = [
        pltpu.VMEM((2, 4 * C, 2 * W), jnp.bfloat16),
        pltpu.VMEM((2, 8 * C2, 2 * W), jnp.bfloat16),
        pltpu.VMEM((2, 2, 2 * rows, C2, 2 * W), jnp.bfloat16),
        pltpu.SemaphoreType.DMA((2, 2)),
    ]

    def upsample(core, edge, first, second, pixels):
        args = (s, u, slots, spread, first) + (() if edge else (second,))
        specs = [VMEM] * len(args)
        aliases = {}
        if pixels is not None:
            aliases = {len(args): 0}
            args, specs = args + (pixels,), specs + [ANY]
        flops = 9_000_000_000 if core else 900_000_000
        kernel = functools.partial(upsample_kernel, core, edge)
        return call(kernel, out, specs, flops, ANY, scratch_shapes=scratch, input_output_aliases=aliases)(*args)

    pixels = upsample(1, None, odd1, odd2, None)
    pixels = upsample(0, True, even1, even2, pixels)
    return upsample(0, False, even1, even2, pixels)


def solution(mesh):
    placed = (P("dp", "tm", "rows", None, None), P(), P(), P(), P())
    return jax.shard_map(
        on_device,
        mesh=mesh,
        in_specs=placed,
        out_specs=P("dp", "tm", "rows", None, None),
        check_vma=False,
    )
```

```python
import functools

import jax
import jax.numpy as jnp
from jax import lax
from jax.experimental import pallas as pl
from jax.experimental.pallas import tpu as pltpu
from jax.sharding import PartitionSpec as P

C = 192
C2 = 96
W = 128
VMEM_LIMIT = 16 * 1024 * 1024
AXES = ("dp", "tm", "rows")


def activate(x, gain):
    meansq = jnp.mean(x * x, axis=0, keepdims=True)
    g = x * lax.rsqrt(meansq + 1e-06) * gain
    return (g * jax.nn.sigmoid(g)).astype(jnp.bfloat16)


def column(row):
    i = lax.broadcasted_iota(jnp.int32, (C, C), 0)
    j = lax.broadcasted_iota(jnp.int32, (C, C), 1)
    return jnp.sum(jnp.where(i == j, row, 0.0), axis=1, keepdims=True)


def pair(ref, frame, row):
    return jnp.concatenate([ref[0, frame, row], ref[1, frame, row]], axis=1)


def shifted(p, by):
    lane = lax.broadcasted_iota(jnp.int32, (p.shape[0], W), 1)
    edge = 0 if by == 1 else W - 1
    halves = []
    for t in range(2):
        moved = pltpu.roll(p[:, t * W : (t + 1) * W], by % W, 1)
        halves.append(jnp.where(lane == edge, 0.0, moved))
    return jnp.concatenate(halves, axis=1)


def conv_terms(acts, w_ref, row_out, flip):
    acc = None
    for kt, panels in acts:
        for row in range(2):
            kh = row - row_out + 2
            if 0 <= kh <= 2:
                tap = kt * 3 + jnp.where(flip, 2 - kh, kh)
                term = jnp.dot(w_ref[tap], panels[row], preferred_element_type=jnp.float32)
                acc = term if acc is None else acc + term
    return shifted(acc[:C], 1) + acc[C : 2 * C] + shifted(acc[2 * C :], -1)


def flipped():
    return lax.rem(lax.axis_index("rows"), 2) == 1


def panels(x_ref, flip):
    rows = [jnp.where(flip, 1 - r, r) for r in range(2)]
    return [[pair(x_ref, f, r).astype(jnp.float32) for r in rows] for f in range(2)]


def spread_kernel(spread_ref):
    src = lax.broadcasted_iota(jnp.int32, (2 * W, 2 * W), 0)
    dst = lax.broadcasted_iota(jnp.int32, (2 * W, 2 * W), 1)
    spread_ref[...] = (dst == jnp.where(src < W, 2 * src, 2 * (src - W) + 1)).astype(jnp.bfloat16)


def own_kernel(x_ref, gain_ref, w_ref, spread_ref, s_ref, _):
    flip = flipped()
    gain = column(gain_ref[...])
    xs = panels(x_ref, flip)
    a = [[activate(xs[f][r], gain) for r in range(2)] for f in range(2)]
    for fo in range(2):
        for ro in range(4):
            total = conv_terms([(2 - (fo - fi), a[fi]) for fi in range(fo + 1)], w_ref, ro, flip)
            if ro in (1, 2):
                total = total + xs[fo][ro - 1]
            s_ref[fo, ro] = total


def previous_kernel(core, x_ref, gain_ref, w_ref, s1_ref, uw_ref, *refs):
    s_ref, first_ref, second_ref, u_ref = refs[-4:]
    tm = lax.axis_index("tm")
    flip = flipped()

    @pl.when(lax.rem(tm, 2) == core)
    def _():
        gain = jnp.where(tm > 0, column(gain_ref[...]), 0.0)
        a = [[activate(x, gain) for x in xs] for xs in panels(x_ref, flip)]
        for fo in range(2):
            acts = [(0, a[0]), (1, a[1])] if fo == 0 else [(0, a[1])]
            for ro in range(4):
                total = s1_ref[fo, ro] + conv_terms(acts, w_ref, ro, flip)
                s_ref[fo, ro] = total
                to_ref = first_ref if ro >= 2 else second_ref
                to_ref[fo, ro % 2] = total.astype(jnp.bfloat16)

    @pl.when(lax.rem(tm, 2) != core)
    def _():
        w0, w1, w2 = (uw_ref[jnp.where(flip, 2 - kh, kh)].astype(jnp.float32) for kh in range(3))
        u_ref[0] = jnp.concatenate([w0, w1 + w2], axis=1).astype(jnp.bfloat16)
        u_ref[1] = jnp.concatenate([w0 + w1, w2], axis=1).astype(jnp.bfloat16)


def upsample_kernel(core, edge, s_ref, u_ref, slot_ref, spread_ref, first_ref, *refs):
    out_ref, h_ref, b_ref, buf_ref, sem = refs[-5:]
    second_ref = refs[0]
    row, rows = lax.axis_index("rows"), lax.axis_size("rows")
    mine = lax.rem(lax.axis_index("tm"), 2) == core
    at_edge = jnp.logical_or(row == 0, row == rows - 1)

    if edge is not None:
        mine = jnp.logical_and(mine, at_edge == edge)

    @pl.when(mine)
    def _():
        flip = flipped()
        spread = spread_ref[...]
        keep = []
        for t in range(2):
            hit = slot_ref[...] == lax.axis_index("dp") * 2 + t
            keep.append(jnp.max(jnp.where(hit, 1.0, 0.0), axis=1, keepdims=True))
        copies = []
        for f in range(2):
            for ro in range(4):
                total = s_ref[f, ro]
                if ro >= 2 or not edge:
                    got = (first_ref if ro >= 2 else second_ref)[f, 1 - ro % 2]
                    total = total + got.astype(jnp.float32)
                if edge is None and ro < 2:
                    alone = s_ref[f, ro] if ro == 1 else jnp.zeros_like(total)
                    total = jnp.where(at_edge, alone, total)
                elif edge and ro == 0:
                    total = jnp.zeros_like(total)
                h_ref[f, ro * C : (ro + 1) * C] = total.astype(jnp.bfloat16)
            for q in range(2):
                for parity in range(2):
                    low = (q + parity) * C
                    total = jnp.dot(u_ref[parity], h_ref[f, low : low + 2 * C], preferred_element_type=jnp.float32)
                    k0, k1, k2 = total[:C2], total[C2 : 2 * C2], total[2 * C2 :]
                    even = (shifted(k0, 1) + k1 + k2).astype(jnp.bfloat16)
                    odd = (k0 + k1 + shifted(k2, -1)).astype(jnp.bfloat16)
                    for t in range(2):
                        at = (t * 4 + 2 * q + parity) * C2
                        b_ref[f, at : at + C2, :W] = even[:, t * W : (t + 1) * W]
                        b_ref[f, at : at + C2, W:] = odd[:, t * W : (t + 1) * W]
        for f in range(2):
            for t in range(2):
                wide = jnp.dot(b_ref[f, t * 4 * C2 : (t + 1) * 4 * C2], spread, preferred_element_type=jnp.float32)
                wide = (wide * keep[t]).astype(jnp.bfloat16)
                for at_row in range(4):
                    to_row = jnp.where(flip, 3 - at_row, at_row)
                    buf_ref[f, t, to_row] = wide[at_row * C2 : (at_row + 1) * C2]
            for t in range(2):
                copy = pltpu.make_async_copy(buf_ref.at[f, t], out_ref.at[t, f], sem.at[f, t])
                copy.start()
                copies.append(copy)
        for copy in copies:
            copy.wait()


VMEM = pl.BlockSpec(memory_space=pltpu.VMEM)
ANY = pl.BlockSpec(memory_space=pl.ANY)


def call(kernel, out_shape, in_specs, flops, out_spec=VMEM, **more):
    out_specs = jax.tree.map(lambda _: out_spec, out_shape)
    return pl.pallas_call(
        kernel,
        out_shape=out_shape,
        in_specs=in_specs,
        out_specs=out_specs,
        compiler_params=pltpu.CompilerParams(vmem_limit_bytes=VMEM_LIMIT),
        cost_estimate=pl.CostEstimate(flops=flops, bytes_accessed=4_000_000, transcendentals=0),
        **more,
    )


def swap(value, partner):
    n_dp, n_tm, n_rows = (lax.axis_size(a) for a in AXES)

    def index(d, t, r):
        return (d * n_tm + t) * n_rows + r

    places = [(d, t, r) for d in range(n_dp) for t in range(n_tm) for r in range(n_rows)]
    return lax.ppermute(value, AXES, [(index(*p), index(*partner(*p))) for p in places])


def on_device(latents, slot_tile, norm_gain, conv_weight, up_weight):
    own_tiles, frames, rows = latents.shape[:3]
    n_dp, n_tm, n_rows = (lax.axis_size(a) for a in AXES)
    slots = slot_tile.reshape(1, -1)
    gain = norm_gain.reshape(1, C)
    w = conv_weight.reshape(9, 3 * C, C)
    uw = up_weight.reshape(3, 3 * C2, C)

    def idle(phase):
        return lambda d: (d ^ 1) if phase == 0 else ((d + 1) % n_dp if d % 2 else (d - 1) % n_dp)

    def across_chips(d, t, r):
        if t in (0, n_tm - 1):
            return idle(0)(d), t, r
        return d, (t + 1 if t % 2 else t - 1), r

    def rows_swap(phase, core):
        def partner(d, t, r):
            if t % 2 != core:
                return idle(phase)(d), t, r
            if phase == 0:
                return d, t, r ^ 1
            return d, t, ((r + 1) % n_rows if r % 2 else (r - 1) % n_rows)

        return partner

    part = jax.ShapeDtypeStruct((2, 4, C, 2 * W), jnp.float32)
    half = jax.ShapeDtypeStruct((2, 2, C, 2 * W), jnp.bfloat16)

    from_chip = swap(latents, lambda d, t, r: (d, t ^ 1, r))
    from_z = swap(latents, across_chips)
    square = jax.ShapeDtypeStruct((2 * W, 2 * W), jnp.bfloat16)
    spread = call(spread_kernel, square, [], 1_500_000_000)()
    s1, spread = call(own_kernel, (part, square), [VMEM] * 4, 1_020_000_000, input_output_aliases={3: 1})(
        latents, gain, w, spread
    )
    specs = [VMEM] * 5
    wide = jax.ShapeDtypeStruct((2, 3 * C2, 2 * C), jnp.bfloat16)
    s, odd1, odd2, u = call(
        functools.partial(previous_kernel, 1), (part, half, half, wide), specs, 1_020_000_000
    )(from_chip, gain, w, s1, uw)
    odd1 = swap(odd1, rows_swap(0, 1))
    odd2 = swap(odd2, rows_swap(1, 1))
    s, even1, even2, u = call(
        functools.partial(previous_kernel, 0),
        (part, half, half, wide),
        specs + [VMEM] * 2,
        1_020_000_000,
        input_output_aliases={5: 0, 6: 3},
    )(from_z, gain, w, s1, uw, s, u)
    even1 = swap(even1, rows_swap(0, 0))
    even2 = swap(even2, rows_swap(1, 0))
    out = jax.ShapeDtypeStruct((own_tiles, frames, 2 * rows, C2, 2 * W), jnp.bfloat16)
    scratch = [
        pltpu.VMEM((2, 4 * C, 2 * W), jnp.bfloat16),
        pltpu.VMEM((2, 8 * C2, 2 * W), jnp.bfloat16),
        pltpu.VMEM((2, 2, 2 * rows, C2, 2 * W), jnp.bfloat16),
        pltpu.SemaphoreType.DMA((2, 2)),
    ]

    def upsample(core, edge, first, second, pixels):
        args = (s, u, slots, spread, first) + (() if edge else (second,))
        specs = [VMEM] * len(args)
        aliases = {}
        if pixels is not None:
            aliases = {len(args): 0}
            args, specs = args + (pixels,), specs + [ANY]
        flops = 9_000_000_000 if core else 900_000_000
        kernel = functools.partial(upsample_kernel, core, edge)
        return call(kernel, out, specs, flops, ANY, scratch_shapes=scratch, input_output_aliases=aliases)(*args)

    pixels = upsample(1, None, odd1, odd2, None)
    pixels = upsample(0, True, even1, even2, pixels)
    return upsample(0, False, even1, even2, pixels)


def solution(mesh):
    placed = (P("dp", "tm", "rows", None, None), P(), P(), P(), P())
    return jax.shard_map(
        on_device,
        mesh=mesh,
        in_specs=placed,
        out_specs=P("dp", "tm", "rows", None, None),
        check_vma=False,
    )
```

```python
import functools

import jax
import jax.numpy as jnp
from jax import lax
from jax.experimental import pallas as pl
from jax.experimental.pallas import tpu as pltpu
from jax.sharding import PartitionSpec as P

C = 192
C2 = 96
W = 128
VMEM_LIMIT = 16 * 1024 * 1024
AXES = ("dp", "tm", "rows")


def activate(x, gain):
    meansq = jnp.mean(x * x, axis=0, keepdims=True)
    g = x * lax.rsqrt(meansq + 1e-06) * gain
    return (g * jax.nn.sigmoid(g)).astype(jnp.bfloat16)


def column(row):
    i = lax.broadcasted_iota(jnp.int32, (C, C), 0)
    j = lax.broadcasted_iota(jnp.int32, (C, C), 1)
    return jnp.sum(jnp.where(i == j, row, 0.0), axis=1, keepdims=True)


def pair(ref, frame, row):
    return jnp.concatenate([ref[0, frame, row], ref[1, frame, row]], axis=1)


def shifted(p, by):
    lane = lax.broadcasted_iota(jnp.int32, (p.shape[0], W), 1)
    edge = 0 if by == 1 else W - 1
    halves = []
    for t in range(2):
        moved = pltpu.roll(p[:, t * W : (t + 1) * W], by % W, 1)
        halves.append(jnp.where(lane == edge, 0.0, moved))
    return jnp.concatenate(halves, axis=1)


def conv_terms(acts, w_ref, row_out, flip):
    acc = None
    for kt, panels in acts:
        for row in range(2):
            kh = row - row_out + 2
            if 0 <= kh <= 2:
                tap = kt * 3 + jnp.where(flip, 2 - kh, kh)
                term = jnp.dot(w_ref[tap], panels[row], preferred_element_type=jnp.float32)
                acc = term if acc is None else acc + term
    return shifted(acc[:C], 1) + acc[C : 2 * C] + shifted(acc[2 * C :], -1)


def flipped():
    return lax.rem(lax.axis_index("rows"), 2) == 1


def panels(x_ref, flip):
    rows = [jnp.where(flip, 1 - r, r) for r in range(2)]
    return [[pair(x_ref, f, r).astype(jnp.float32) for r in rows] for f in range(2)]


def spread_kernel(spread_ref):
    src = lax.broadcasted_iota(jnp.int32, (2 * W, 2 * W), 0)
    dst = lax.broadcasted_iota(jnp.int32, (2 * W, 2 * W), 1)
    spread_ref[...] = (dst == jnp.where(src < W, 2 * src, 2 * (src - W) + 1)).astype(jnp.bfloat16)


def own_kernel(x_ref, gain_ref, w_ref, spread_ref, s_ref, _):
    flip = flipped()
    gain = column(gain_ref[...])
    xs = panels(x_ref, flip)
    a = [[activate(xs[f][r], gain) for r in range(2)] for f in range(2)]
    for fo in range(2):
        for ro in range(4):
            total = conv_terms([(2 - (fo - fi), a[fi]) for fi in range(fo + 1)], w_ref, ro, flip)
            if ro in (1, 2):
                total = total + xs[fo][ro - 1]
            s_ref[fo, ro] = total


def previous_kernel(core, x_ref, gain_ref, w_ref, s1_ref, uw_ref, *refs):
    s_ref, first_ref, second_ref, u_ref = refs[-4:]
    tm = lax.axis_index("tm")
    flip = flipped()

    @pl.when(lax.rem(tm, 2) == core)
    def _():
        gain = jnp.where(tm > 0, column(gain_ref[...]), 0.0)
        a = [[activate(x, gain) for x in xs] for xs in panels(x_ref, flip)]
        for fo in range(2):
            acts = [(0, a[0]), (1, a[1])] if fo == 0 else [(0, a[1])]
            for ro in range(4):
                total = s1_ref[fo, ro] + conv_terms(acts, w_ref, ro, flip)
                s_ref[fo, ro] = total
                to_ref = first_ref if ro >= 2 else second_ref
                to_ref[fo, ro % 2] = total.astype(jnp.bfloat16)

    @pl.when(lax.rem(tm, 2) != core)
    def _():
        w0, w1, w2 = (uw_ref[jnp.where(flip, 2 - kh, kh)].astype(jnp.float32) for kh in range(3))
        u_ref[0] = jnp.concatenate([w0, w1 + w2], axis=1).astype(jnp.bfloat16)
        u_ref[1] = jnp.concatenate([w0 + w1, w2], axis=1).astype(jnp.bfloat16)


def hidden_row(s_ref, f, ro, got_ref):
    total = s_ref[f, ro]
    if got_ref is not None:
        total = total + got_ref[f, 1 - ro % 2].astype(jnp.float32)
    return total


def upsample(h_ref, u_ref, slot_ref, spread_ref, b_ref, buf_ref, out_ref, sem, todo, flip):
    spread = spread_ref[...]
    n = len(todo)
    for f in range(2):
        for i, at_row in enumerate(todo):
            low = (at_row // 2 + at_row % 2) * C
            total = jnp.dot(u_ref[at_row % 2], h_ref[f, low : low + 2 * C], preferred_element_type=jnp.float32)
            k0, k1, k2 = total[:C2], total[C2 : 2 * C2], total[2 * C2 :]
            even = (shifted(k0, 1) + k1 + k2).astype(jnp.bfloat16)
            odd = (k0 + k1 + shifted(k2, -1)).astype(jnp.bfloat16)
            for t in range(2):
                at = (t * n + i) * C2
                b_ref[f, at : at + C2, :W] = even[:, t * W : (t + 1) * W]
                b_ref[f, at : at + C2, W:] = odd[:, t * W : (t + 1) * W]
    copies = []
    for f in range(2):
        for t in range(2):
            hit = slot_ref[...] == lax.axis_index("dp") * 2 + t
            keep = jnp.max(jnp.where(hit, 1.0, 0.0), axis=1, keepdims=True)
            wide = jnp.dot(b_ref[f, t * n * C2 : (t + 1) * n * C2], spread, preferred_element_type=jnp.float32)
            wide = (wide * keep).astype(jnp.bfloat16)
            for i in range(n):
                buf_ref[f, t, jnp.where(flip, n - 1 - i, i)] = wide[i * C2 : (i + 1) * C2]
        if out_ref is not None:
            for t in range(2):
                copies.append(out_copy(buf_ref, out_ref, sem, f, t, todo, flip))
                copies[-1].start()
    for copy in copies:
        copy.wait()


def out_copy(buf_ref, out_ref, sem, f, t, todo, flip):
    first, n = jnp.where(flip, 3 - todo[-1], todo[0]), len(todo)
    return pltpu.make_async_copy(buf_ref.at[f, t, pl.ds(0, n)], out_ref.at[t, f, pl.ds(first, n)], sem.at[f, t])


def place(core):
    row = lax.axis_index("rows")
    mine = lax.rem(lax.axis_index("tm"), 2) == core
    return mine, jnp.logical_or(row == 0, row == lax.axis_size("rows") - 1)


def odd_kernel(s_ref, u_ref, slot_ref, spread_ref, first_ref, second_ref, out_ref, h_ref, b_ref, buf_ref, sem):
    mine, edge = place(1)

    @pl.when(mine)
    def _():
        for f in range(2):
            for ro in range(4):
                total = hidden_row(s_ref, f, ro, first_ref if ro >= 2 else second_ref)
                if ro < 2:
                    alone = s_ref[f, ro] if ro == 1 else jnp.zeros_like(total)
                    total = jnp.where(edge, alone, total)
                h_ref[f, ro * C : (ro + 1) * C] = total.astype(jnp.bfloat16)
        upsample(h_ref, u_ref, slot_ref, spread_ref, b_ref, buf_ref, out_ref, sem, (0, 1, 2, 3), flipped())


def even_first_kernel(
    s_ref, u_ref, slot_ref, spread_ref, first_ref, _, out_ref, h_ref, kept_ref, b_ref, buf_ref, sem
):
    mine, edge = place(0)

    def lower():
        for f in range(2):
            for ro in (2, 3):
                h_ref[f, ro * C : (ro + 1) * C] = hidden_row(s_ref, f, ro, first_ref).astype(jnp.bfloat16)

    @pl.when(jnp.logical_and(mine, edge))
    def _():
        lower()
        for f in range(2):
            h_ref[f, :C] = jnp.zeros((C, 2 * W), jnp.bfloat16)
            h_ref[f, C : 2 * C] = hidden_row(s_ref, f, 1, None).astype(jnp.bfloat16)
        upsample(h_ref, u_ref, slot_ref, spread_ref, b_ref, buf_ref, out_ref, sem, (0, 1, 2, 3), flipped())

    @pl.when(jnp.logical_and(mine, jnp.logical_not(edge)))
    def _():
        lower()
        upsample(h_ref, u_ref, slot_ref, spread_ref, b_ref, kept_ref, None, sem, (3,), flipped())


def even_second_kernel(
    s_ref, u_ref, slot_ref, spread_ref, _, second_ref, low_ref, kept_ref, __, out_ref, h_ref, b_ref, buf_ref, sem, kept_sem
):
    mine, edge = place(0)

    @pl.when(jnp.logical_and(mine, jnp.logical_not(edge)))
    def _():
        kept = [out_copy(kept_ref, out_ref, kept_sem, f, t, (3,), flipped()) for f in range(2) for t in range(2)]
        for copy in kept:
            copy.start()
        for f in range(2):
            for ro in range(2):
                h_ref[f, ro * C : (ro + 1) * C] = hidden_row(s_ref, f, ro, second_ref).astype(jnp.bfloat16)
            h_ref[f, 2 * C : 3 * C] = low_ref[f, 2 * C : 3 * C]
        upsample(h_ref, u_ref, slot_ref, spread_ref, b_ref, buf_ref, out_ref, sem, (0, 1, 2), flipped())
        for copy in kept:
            copy.wait()


VMEM = pl.BlockSpec(memory_space=pltpu.VMEM)
ANY = pl.BlockSpec(memory_space=pl.ANY)


def call(kernel, out_shape, in_specs, flops, out_spec=VMEM, **more):
    out_specs = out_spec if isinstance(out_spec, tuple) else jax.tree.map(lambda _: out_spec, out_shape)
    return pl.pallas_call(
        kernel,
        out_shape=out_shape,
        in_specs=in_specs,
        out_specs=out_specs,
        compiler_params=pltpu.CompilerParams(vmem_limit_bytes=VMEM_LIMIT),
        cost_estimate=pl.CostEstimate(flops=flops, bytes_accessed=4_000_000, transcendentals=0),
        **more,
    )


def swap(value, partner):
    n_dp, n_tm, n_rows = (lax.axis_size(a) for a in AXES)

    def index(d, t, r):
        return (d * n_tm + t) * n_rows + r

    places = [(d, t, r) for d in range(n_dp) for t in range(n_tm) for r in range(n_rows)]
    return lax.ppermute(value, AXES, [(index(*p), index(*partner(*p))) for p in places])


def on_device(latents, slot_tile, norm_gain, conv_weight, up_weight):
    own_tiles, frames, rows = latents.shape[:3]
    n_dp, n_tm, n_rows = (lax.axis_size(a) for a in AXES)
    slots = slot_tile.reshape(1, -1)
    gain = norm_gain.reshape(1, C)
    w = conv_weight.reshape(9, 3 * C, C)
    uw = up_weight.reshape(3, 3 * C2, C)

    def idle(phase):
        return lambda d: (d ^ 1) if phase == 0 else ((d + 1) % n_dp if d % 2 else (d - 1) % n_dp)

    def across_chips(d, t, r):
        if t in (0, n_tm - 1):
            return idle(0)(d), t, r
        return d, (t + 1 if t % 2 else t - 1), r

    def rows_swap(phase, core):
        def partner(d, t, r):
            if t % 2 != core:
                return idle(phase)(d), t, r
            if phase == 0:
                return d, t, r ^ 1
            return d, t, ((r + 1) % n_rows if r % 2 else (r - 1) % n_rows)

        return partner

    def shape(*dims, dtype=jnp.bfloat16):
        return jax.ShapeDtypeStruct(dims, dtype)

    part = jax.ShapeDtypeStruct((2, 4, C, 2 * W), jnp.float32)
    half = jax.ShapeDtypeStruct((2, 2, C, 2 * W), jnp.bfloat16)

    from_chip = swap(latents, lambda d, t, r: (d, t ^ 1, r))
    from_z = swap(latents, across_chips)
    square = jax.ShapeDtypeStruct((2 * W, 2 * W), jnp.bfloat16)
    spread = call(spread_kernel, square, [], 1_500_000_000)()
    s1, spread = call(own_kernel, (part, square), [VMEM] * 4, 1_020_000_000, input_output_aliases={3: 1})(
        latents, gain, w, spread
    )
    specs = [VMEM] * 5
    wide = jax.ShapeDtypeStruct((2, 3 * C2, 2 * C), jnp.bfloat16)
    s, odd1, odd2, u = call(
        functools.partial(previous_kernel, 1), (part, half, half, wide), specs, 1_020_000_000
    )(from_chip, gain, w, s1, uw)
    odd1 = swap(odd1, rows_swap(0, 1))
    odd2 = swap(odd2, rows_swap(1, 1))
    s, even1, even2, u = call(
        functools.partial(previous_kernel, 0),
        (part, half, half, wide),
        specs + [VMEM] * 2,
        1_020_000_000,
        input_output_aliases={5: 0, 6: 3},
    )(from_z, gain, w, s1, uw, s, u)
    even1 = swap(even1, rows_swap(0, 0))
    even2 = swap(even2, rows_swap(1, 0))
    out = jax.ShapeDtypeStruct((own_tiles, frames, 2 * rows, C2, 2 * W), jnp.bfloat16)
    rows_of = shape(2, 4 * C, 2 * W)
    scratch = [
        pltpu.VMEM((2, 8 * C2, 2 * W), jnp.bfloat16),
        pltpu.VMEM((2, 2, 2 * rows, C2, 2 * W), jnp.bfloat16),
        pltpu.SemaphoreType.DMA((2, 2)),
    ]
    ahead = pltpu.VMEM(rows_of.shape, rows_of.dtype)
    common = (s, u, slots, spread)
    pixels = call(odd_kernel, out, [VMEM] * 6, 9_000_000_000, ANY, scratch_shapes=[ahead] + scratch)(
        *common, odd1, odd2
    )
    pixels, lower, kept = call(
        even_first_kernel,
        (out, rows_of, shape(2, 2, 1, C2, 2 * W)),
        [VMEM] * 5 + [ANY],
        900_000_000,
        (ANY, VMEM, VMEM),
        scratch_shapes=scratch,
        input_output_aliases={5: 0},
    )(*common, even1, pixels)
    return call(
        even_second_kernel,
        out,
        [VMEM] * 8 + [ANY],
        700_000_000,
        ANY,
        scratch_shapes=[ahead] + scratch + [pltpu.SemaphoreType.DMA((2, 2))],
        input_output_aliases={8: 0},
    )(*common, even1, even2, lower, kept, pixels)


def solution(mesh):
    placed = (P("dp", "tm", "rows", None, None), P(), P(), P(), P())
    return jax.shard_map(
        on_device,
        mesh=mesh,
        in_specs=placed,
        out_specs=P("dp", "tm", "rows", None, None),
        check_vma=False,
    )
```

```python
import functools

import jax
import jax.numpy as jnp
from jax import lax
from jax.experimental import pallas as pl
from jax.experimental.pallas import tpu as pltpu
from jax.sharding import PartitionSpec as P

C = 192
C2 = 96
W = 128
VMEM_LIMIT = 16 * 1024 * 1024
AXES = ("dp", "tm", "rows")


def activate(x, gain):
    meansq = jnp.mean(x * x, axis=0, keepdims=True)
    g = x * lax.rsqrt(meansq + 1e-06) * gain
    return (g * jax.nn.sigmoid(g)).astype(jnp.bfloat16)


def column(row):
    i = lax.broadcasted_iota(jnp.int32, (C, C), 0)
    j = lax.broadcasted_iota(jnp.int32, (C, C), 1)
    return jnp.sum(jnp.where(i == j, row, 0.0), axis=1, keepdims=True)


def pair(ref, frame, row):
    return jnp.concatenate([ref[0, frame, row], ref[1, frame, row]], axis=1)


def shifted(p, by):
    lane = lax.broadcasted_iota(jnp.int32, (p.shape[0], W), 1)
    edge = 0 if by == 1 else W - 1
    halves = []
    for t in range(2):
        moved = pltpu.roll(p[:, t * W : (t + 1) * W], by % W, 1)
        halves.append(jnp.where(lane == edge, 0.0, moved))
    return jnp.concatenate(halves, axis=1)


def conv_terms(acts, w_ref, row_out, flip):
    acc = None
    for kt, panels in acts:
        for row in range(2):
            kh = row - row_out + 2
            if 0 <= kh <= 2:
                tap = kt * 3 + jnp.where(flip, 2 - kh, kh)
                term = jnp.dot(w_ref[tap], panels[row], preferred_element_type=jnp.float32)
                acc = term if acc is None else acc + term
    return columns(acc)


def columns(acc):
    return shifted(acc[:C], 1) + acc[C : 2 * C] + shifted(acc[2 * C :], -1)


def flipped():
    return lax.rem(lax.axis_index("rows"), 2) == 1


def panels(x_ref, flip):
    rows = [jnp.where(flip, 1 - r, r) for r in range(2)]
    return [[pair(x_ref, f, r).astype(jnp.float32) for r in rows] for f in range(2)]


def spread_kernel(spread_ref):
    src = lax.broadcasted_iota(jnp.int32, (2 * W, 2 * W), 0)
    dst = lax.broadcasted_iota(jnp.int32, (2 * W, 2 * W), 1)
    spread_ref[...] = (dst == jnp.where(src < W, 2 * src, 2 * (src - W) + 1)).astype(jnp.bfloat16)


def own_kernel(x_ref, gain_ref, w_ref, spread_ref, s_ref, _):
    flip = flipped()
    gain = column(gain_ref[...])
    xs = panels(x_ref, flip)
    a = [[activate(xs[f][r], gain) for r in range(2)] for f in range(2)]
    for fo in range(2):
        for ro in range(4):
            total = conv_terms([(2 - (fo - fi), a[fi]) for fi in range(fo + 1)], w_ref, ro, flip)
            if ro in (1, 2):
                total = total + xs[fo][ro - 1]
            s_ref[fo, ro] = total


def previous_kernel(core, x_ref, gain_ref, w_ref, s1_ref, uw_ref, *refs):
    s_ref, first_ref, second_ref, u_ref = refs[-4:] if core == 0 else refs[:4]
    four_ref = refs[0] if core == 0 else refs[4]
    tm = lax.axis_index("tm")
    flip = flipped()

    @pl.when(lax.rem(tm, 2) == core)
    def _():
        gain = jnp.where(tm > 0, column(gain_ref[...]), 0.0)
        a = [[activate(x, gain) for x in xs] for xs in panels(x_ref, flip)]
        for fo in range(2):
            acts = [(0, a[0]), (1, a[1])] if fo == 0 else [(0, a[1])]
            for ro in range(4):
                if core == 0 and fo == 0 and ro in (1, 2):
                    four = jnp.concatenate(a[0] + a[1], axis=0)
                    terms = columns(jnp.dot(four_ref[ro - 1], four, preferred_element_type=jnp.float32))
                else:
                    terms = conv_terms(acts, w_ref, ro, flip)
                total = s1_ref[fo, ro] + terms
                s_ref[fo, ro] = total
                to_ref = first_ref if ro >= 2 else second_ref
                to_ref[fo, ro % 2] = total.astype(jnp.bfloat16)

    @pl.when(lax.rem(tm, 2) != core)
    def _():
        w0, w1, w2 = (uw_ref[jnp.where(flip, 2 - kh, kh)].astype(jnp.float32) for kh in range(3))
        u_ref[0] = jnp.concatenate([w0, w1 + w2], axis=1).astype(jnp.bfloat16)
        u_ref[1] = jnp.concatenate([w0 + w1, w2], axis=1).astype(jnp.bfloat16)
        if core == 1:
            for ro in (1, 2):
                khs = [row - ro + 2 for row in range(2)]
                taps = [w_ref[kt * 3 + jnp.where(flip, 2 - kh, kh)] for kt in range(2) for kh in khs]
                four_ref[ro - 1] = jnp.concatenate(taps, axis=1)


def hidden_row(s_ref, f, ro, got_ref):
    total = s_ref[f, ro]
    if got_ref is not None:
        total = total + got_ref[f, 1 - ro % 2].astype(jnp.float32)
    return total


def upsample(h_ref, u_ref, slot_ref, spread_ref, b_ref, buf_ref, out_ref, sem, todo, flip):
    spread = spread_ref[...]
    n = len(todo)
    for f in range(2):
        for i, at_row in enumerate(todo):
            low = (at_row // 2 + at_row % 2) * C
            total = jnp.dot(u_ref[at_row % 2], h_ref[f, low : low + 2 * C], preferred_element_type=jnp.float32)
            k0, k1, k2 = total[:C2], total[C2 : 2 * C2], total[2 * C2 :]
            even = (shifted(k0, 1) + k1 + k2).astype(jnp.bfloat16)
            odd = (k0 + k1 + shifted(k2, -1)).astype(jnp.bfloat16)
            for t in range(2):
                at = (t * n + i) * C2
                b_ref[f, at : at + C2, :W] = even[:, t * W : (t + 1) * W]
                b_ref[f, at : at + C2, W:] = odd[:, t * W : (t + 1) * W]
    copies = []
    for f in range(2):
        for t in range(2):
            hit = slot_ref[...] == lax.axis_index("dp") * 2 + t
            keep = jnp.max(jnp.where(hit, 1.0, 0.0), axis=1, keepdims=True)
            wide = jnp.dot(b_ref[f, t * n * C2 : (t + 1) * n * C2], spread, preferred_element_type=jnp.float32)
            wide = (wide * keep).astype(jnp.bfloat16)
            for i in range(n):
                buf_ref[f, t, jnp.where(flip, n - 1 - i, i)] = wide[i * C2 : (i + 1) * C2]
        if out_ref is not None:
            for t in range(2):
                copies.append(out_copy(buf_ref, out_ref, sem, f, t, todo, flip))
                copies[-1].start()
    for copy in copies:
        copy.wait()


def out_copy(buf_ref, out_ref, sem, f, t, todo, flip):
    first, n = jnp.where(flip, 3 - todo[-1], todo[0]), len(todo)
    return pltpu.make_async_copy(buf_ref.at[f, t, pl.ds(0, n)], out_ref.at[t, f, pl.ds(first, n)], sem.at[f, t])


def place(core):
    row = lax.axis_index("rows")
    mine = lax.rem(lax.axis_index("tm"), 2) == core
    return mine, jnp.logical_or(row == 0, row == lax.axis_size("rows") - 1)


def odd_kernel(s_ref, u_ref, slot_ref, spread_ref, first_ref, second_ref, out_ref, h_ref, b_ref, buf_ref, sem):
    mine, edge = place(1)

    @pl.when(mine)
    def _():
        for f in range(2):
            for ro in range(4):
                total = hidden_row(s_ref, f, ro, first_ref if ro >= 2 else second_ref)
                if ro < 2:
                    alone = s_ref[f, ro] if ro == 1 else jnp.zeros_like(total)
                    total = jnp.where(edge, alone, total)
                h_ref[f, ro * C : (ro + 1) * C] = total.astype(jnp.bfloat16)
        upsample(h_ref, u_ref, slot_ref, spread_ref, b_ref, buf_ref, out_ref, sem, (0, 1, 2, 3), flipped())


def even_first_kernel(
    s_ref, u_ref, slot_ref, spread_ref, first_ref, _, out_ref, h_ref, kept_ref, b_ref, buf_ref, sem
):
    mine, edge = place(0)

    def lower():
        for f in range(2):
            for ro in (2, 3):
                h_ref[f, ro * C : (ro + 1) * C] = hidden_row(s_ref, f, ro, first_ref).astype(jnp.bfloat16)

    @pl.when(jnp.logical_and(mine, edge))
    def _():
        lower()
        for f in range(2):
            h_ref[f, :C] = jnp.zeros((C, 2 * W), jnp.bfloat16)
            h_ref[f, C : 2 * C] = hidden_row(s_ref, f, 1, None).astype(jnp.bfloat16)
        upsample(h_ref, u_ref, slot_ref, spread_ref, b_ref, buf_ref, out_ref, sem, (0, 1, 2, 3), flipped())

    @pl.when(jnp.logical_and(mine, jnp.logical_not(edge)))
    def _():
        lower()
        upsample(h_ref, u_ref, slot_ref, spread_ref, b_ref, kept_ref, None, sem, (3,), flipped())


def even_second_kernel(
    s_ref, u_ref, slot_ref, spread_ref, _, second_ref, low_ref, kept_ref, __, out_ref, h_ref, b_ref, buf_ref, sem, kept_sem
):
    mine, edge = place(0)

    @pl.when(jnp.logical_and(mine, jnp.logical_not(edge)))
    def _():
        kept = [out_copy(kept_ref, out_ref, kept_sem, f, t, (3,), flipped()) for f in range(2) for t in range(2)]
        for copy in kept:
            copy.start()
        for f in range(2):
            for ro in range(2):
                h_ref[f, ro * C : (ro + 1) * C] = hidden_row(s_ref, f, ro, second_ref).astype(jnp.bfloat16)
            h_ref[f, 2 * C : 3 * C] = low_ref[f, 2 * C : 3 * C]
        upsample(h_ref, u_ref, slot_ref, spread_ref, b_ref, buf_ref, out_ref, sem, (0, 1, 2), flipped())
        for copy in kept:
            copy.wait()


VMEM = pl.BlockSpec(memory_space=pltpu.VMEM)
ANY = pl.BlockSpec(memory_space=pl.ANY)


def call(kernel, out_shape, in_specs, flops, out_spec=VMEM, **more):
    out_specs = out_spec if isinstance(out_spec, tuple) else jax.tree.map(lambda _: out_spec, out_shape)
    return pl.pallas_call(
        kernel,
        out_shape=out_shape,
        in_specs=in_specs,
        out_specs=out_specs,
        compiler_params=pltpu.CompilerParams(vmem_limit_bytes=VMEM_LIMIT),
        cost_estimate=pl.CostEstimate(flops=flops, bytes_accessed=4_000_000, transcendentals=0),
        **more,
    )


def swap(value, partner):
    n_dp, n_tm, n_rows = (lax.axis_size(a) for a in AXES)

    def index(d, t, r):
        return (d * n_tm + t) * n_rows + r

    places = [(d, t, r) for d in range(n_dp) for t in range(n_tm) for r in range(n_rows)]
    return lax.ppermute(value, AXES, [(index(*p), index(*partner(*p))) for p in places])


def on_device(latents, slot_tile, norm_gain, conv_weight, up_weight):
    own_tiles, frames, rows = latents.shape[:3]
    n_dp, n_tm, n_rows = (lax.axis_size(a) for a in AXES)
    slots = slot_tile.reshape(1, -1)
    gain = norm_gain.reshape(1, C)
    w = conv_weight.reshape(9, 3 * C, C)
    uw = up_weight.reshape(3, 3 * C2, C)

    def idle(phase):
        return lambda d: (d ^ 1) if phase == 0 else ((d + 1) % n_dp if d % 2 else (d - 1) % n_dp)

    def across_chips(d, t, r):
        if t in (0, n_tm - 1):
            return idle(0)(d), t, r
        return d, (t + 1 if t % 2 else t - 1), r

    def rows_swap(phase, core):
        def partner(d, t, r):
            if t % 2 != core:
                return idle(1 - phase)(d), t, r
            if phase == 0:
                return d, t, r ^ 1
            return d, t, ((r + 1) % n_rows if r % 2 else (r - 1) % n_rows)

        return partner

    def shape(*dims, dtype=jnp.bfloat16):
        return jax.ShapeDtypeStruct(dims, dtype)

    part = jax.ShapeDtypeStruct((2, 4, C, 2 * W), jnp.float32)
    half = jax.ShapeDtypeStruct((2, 2, C, 2 * W), jnp.bfloat16)

    from_chip = swap(latents, lambda d, t, r: (d, t ^ 1, r))
    from_z = swap(latents, across_chips)
    square = jax.ShapeDtypeStruct((2 * W, 2 * W), jnp.bfloat16)
    spread = call(spread_kernel, square, [], 1_500_000_000)()
    s1, spread = call(own_kernel, (part, square), [VMEM] * 4, 1_020_000_000, input_output_aliases={3: 1})(
        latents, gain, w, spread
    )
    specs = [VMEM] * 5
    wide = jax.ShapeDtypeStruct((2, 3 * C2, 2 * C), jnp.bfloat16)
    s, odd1, odd2, u, four = call(
        functools.partial(previous_kernel, 1), (part, half, half, wide, shape(2, 3 * C, 4 * C)), specs, 1_020_000_000
    )(from_chip, gain, w, s1, uw)
    odd1 = swap(odd1, rows_swap(0, 1))
    odd2 = swap(odd2, rows_swap(1, 1))
    s, even1, even2, u = call(
        functools.partial(previous_kernel, 0),
        (part, half, half, wide),
        specs + [VMEM] * 3,
        1_020_000_000,
        input_output_aliases={6: 0, 7: 3},
    )(from_z, gain, w, s1, uw, four, s, u)
    even1 = swap(even1, rows_swap(0, 0))
    even2 = swap(even2, rows_swap(1, 0))
    out = jax.ShapeDtypeStruct((own_tiles, frames, 2 * rows, C2, 2 * W), jnp.bfloat16)
    rows_of = shape(2, 4 * C, 2 * W)
    scratch = [
        pltpu.VMEM((2, 8 * C2, 2 * W), jnp.bfloat16),
        pltpu.VMEM((2, 2, 2 * rows, C2, 2 * W), jnp.bfloat16),
        pltpu.SemaphoreType.DMA((2, 2)),
    ]
    ahead = pltpu.VMEM(rows_of.shape, rows_of.dtype)
    common = (s, u, slots, spread)
    pixels = call(odd_kernel, out, [VMEM] * 6, 9_000_000_000, ANY, scratch_shapes=[ahead] + scratch)(
        *common, odd1, odd2
    )
    pixels, lower, kept = call(
        even_first_kernel,
        (out, rows_of, shape(2, 2, 1, C2, 2 * W)),
        [VMEM] * 5 + [ANY],
        900_000_000,
        (ANY, VMEM, VMEM),
        scratch_shapes=scratch,
        input_output_aliases={5: 0},
    )(*common, even1, pixels)
    return call(
        even_second_kernel,
        out,
        [VMEM] * 8 + [ANY],
        700_000_000,
        ANY,
        scratch_shapes=[ahead] + scratch + [pltpu.SemaphoreType.DMA((2, 2))],
        input_output_aliases={8: 0},
    )(*common, even1, even2, lower, kept, pixels)


def solution(mesh):
    placed = (P("dp", "tm", "rows", None, None), P(), P(), P(), P())
    return jax.shard_map(
        on_device,
        mesh=mesh,
        in_specs=placed,
        out_specs=P("dp", "tm", "rows", None, None),
        check_vma=False,
    )
```

```python
import functools

import jax
import jax.numpy as jnp
from jax import lax
from jax.experimental import pallas as pl
from jax.experimental.pallas import tpu as pltpu
from jax.sharding import PartitionSpec as P

C = 192
C2 = 96
W = 128
VMEM_LIMIT = 16 * 1024 * 1024
AXES = ("dp", "tm", "rows")


def activate(x, gain):
    meansq = jnp.mean(x * x, axis=0, keepdims=True)
    g = x * lax.rsqrt(meansq + 1e-06) * gain
    return (g * jax.nn.sigmoid(g)).astype(jnp.bfloat16)


def column(row):
    i = lax.broadcasted_iota(jnp.int32, (C, C), 0)
    j = lax.broadcasted_iota(jnp.int32, (C, C), 1)
    return jnp.sum(jnp.where(i == j, row, 0.0), axis=1, keepdims=True)


def pair(ref, frame, row):
    return jnp.concatenate([ref[0, frame, row], ref[1, frame, row]], axis=1)


def shifted(p, by):
    lane = lax.broadcasted_iota(jnp.int32, (p.shape[0], W), 1)
    edge = 0 if by == 1 else W - 1
    halves = []
    for t in range(2):
        moved = pltpu.roll(p[:, t * W : (t + 1) * W], by % W, 1)
        halves.append(jnp.where(lane == edge, 0.0, moved))
    return jnp.concatenate(halves, axis=1)


def conv_terms(acts, w_ref, row_out, flip):
    acc = None
    for kt, panels in acts:
        for row in range(2):
            kh = row - row_out + 2
            if 0 <= kh <= 2:
                tap = kt * 3 + jnp.where(flip, 2 - kh, kh)
                term = jnp.dot(w_ref[tap], panels[row], preferred_element_type=jnp.float32)
                acc = term if acc is None else acc + term
    return columns(acc)


def columns(acc):
    return shifted(acc[:C], 1) + acc[C : 2 * C] + shifted(acc[2 * C :], -1)


def flipped():
    return lax.rem(lax.axis_index("rows"), 2) == 1


def panels(x_ref, flip):
    rows = [jnp.where(flip, 1 - r, r) for r in range(2)]
    return [[pair(x_ref, f, r).astype(jnp.float32) for r in rows] for f in range(2)]


def spread_kernel(spread_ref):
    src = lax.broadcasted_iota(jnp.int32, (2 * W, 2 * W), 0)
    dst = lax.broadcasted_iota(jnp.int32, (2 * W, 2 * W), 1)
    spread_ref[...] = (dst == jnp.where(src < W, 2 * src, 2 * (src - W) + 1)).astype(jnp.bfloat16)


def own_kernel(x_ref, gain_ref, w_ref, spread_ref, s_ref, _):
    flip = flipped()
    gain = column(gain_ref[...])
    xs = panels(x_ref, flip)
    a = [[activate(xs[f][r], gain) for r in range(2)] for f in range(2)]
    for fo in range(2):
        for ro in range(4):
            total = conv_terms([(2 - (fo - fi), a[fi]) for fi in range(fo + 1)], w_ref, ro, flip)
            if ro in (1, 2):
                total = total + xs[fo][ro - 1]
            s_ref[fo, ro] = total


def previous_kernel(core, x_ref, gain_ref, w_ref, s1_ref, uw_ref, *refs):
    s_ref, first_ref, second_ref, u_ref = refs[-4:] if core == 0 else refs[:4]
    four_ref = refs[0] if core == 0 else refs[4]
    tm = lax.axis_index("tm")
    flip = flipped()

    @pl.when(lax.rem(tm, 2) == core)
    def _():
        gain = jnp.where(tm > 0, column(gain_ref[...]), 0.0)
        a = [[activate(x, gain) for x in xs] for xs in panels(x_ref, flip)]
        for fo in range(2):
            acts = [(0, a[0]), (1, a[1])] if fo == 0 else [(0, a[1])]
            for ro in range(4):
                if core == 0 and fo == 0 and ro in (1, 2):
                    four = jnp.concatenate(a[0] + a[1], axis=0)
                    terms = columns(jnp.dot(four_ref[ro - 1], four, preferred_element_type=jnp.float32))
                else:
                    terms = conv_terms(acts, w_ref, ro, flip)
                total = s1_ref[fo, ro] + terms
                s_ref[fo, ro] = total
                to_ref = first_ref if ro >= 2 else second_ref
                to_ref[fo, ro % 2] = total.astype(jnp.bfloat16)

    @pl.when(lax.rem(tm, 2) != core)
    def _():
        w0, w1, w2 = (uw_ref[jnp.where(flip, 2 - kh, kh)].astype(jnp.float32) for kh in range(3))
        u_ref[0] = jnp.concatenate([w0, w1 + w2], axis=1).astype(jnp.bfloat16)
        u_ref[1] = jnp.concatenate([w0 + w1, w2], axis=1).astype(jnp.bfloat16)
        if core == 1:
            for ro in (1, 2):
                khs = [row - ro + 2 for row in range(2)]
                taps = [w_ref[kt * 3 + jnp.where(flip, 2 - kh, kh)] for kt in range(2) for kh in khs]
                four_ref[ro - 1] = jnp.concatenate(taps, axis=1)


def hidden_row(s_ref, f, ro, got_ref):
    total = s_ref[f, ro]
    if got_ref is not None:
        total = total + got_ref[f, 1 - ro % 2].astype(jnp.float32)
    return total


def upsample(h_ref, u_ref, slot_ref, spread_ref, b_ref, buf_ref, out_ref, sem, todo, flip):
    spread = spread_ref[...]
    n = len(todo)
    for f in range(2):
        for i, at_row in enumerate(todo):
            low = (at_row // 2 + at_row % 2) * C
            total = jnp.dot(u_ref[at_row % 2], h_ref[f, low : low + 2 * C], preferred_element_type=jnp.float32)
            k0, k1, k2 = total[:C2], total[C2 : 2 * C2], total[2 * C2 :]
            even = (shifted(k0, 1) + k1 + k2).astype(jnp.bfloat16)
            odd = (k0 + k1 + shifted(k2, -1)).astype(jnp.bfloat16)
            for t in range(2):
                at = (t * n + i) * C2
                b_ref[f, at : at + C2, :W] = even[:, t * W : (t + 1) * W]
                b_ref[f, at : at + C2, W:] = odd[:, t * W : (t + 1) * W]
    copies = []
    for f in range(2):
        for t in range(2):
            hit = slot_ref[...] == lax.axis_index("dp") * 2 + t
            keep = jnp.max(jnp.where(hit, 1.0, 0.0), axis=1, keepdims=True)
            wide = jnp.dot(b_ref[f, t * n * C2 : (t + 1) * n * C2], spread, preferred_element_type=jnp.float32)
            wide = (wide * keep).astype(jnp.bfloat16)
            for i in range(n):
                buf_ref[f, t, jnp.where(flip, n - 1 - i, i)] = wide[i * C2 : (i + 1) * C2]
        if out_ref is not None:
            for t in range(2):
                copies.append(out_copy(buf_ref, out_ref, sem, f, t, todo, flip))
                copies[-1].start(priority=1)
    for copy in copies:
        copy.wait()


def out_copy(buf_ref, out_ref, sem, f, t, todo, flip):
    first, n = jnp.where(flip, 3 - todo[-1], todo[0]), len(todo)
    return pltpu.make_async_copy(buf_ref.at[f, t, pl.ds(0, n)], out_ref.at[t, f, pl.ds(first, n)], sem.at[f, t])


def place(core):
    row = lax.axis_index("rows")
    mine = lax.rem(lax.axis_index("tm"), 2) == core
    return mine, jnp.logical_or(row == 0, row == lax.axis_size("rows") - 1)


def odd_kernel(s_ref, u_ref, slot_ref, spread_ref, first_ref, second_ref, out_ref, h_ref, b_ref, buf_ref, sem):
    mine, edge = place(1)

    @pl.when(mine)
    def _():
        for f in range(2):
            for ro in range(4):
                total = hidden_row(s_ref, f, ro, first_ref if ro >= 2 else second_ref)
                if ro < 2:
                    alone = s_ref[f, ro] if ro == 1 else jnp.zeros_like(total)
                    total = jnp.where(edge, alone, total)
                h_ref[f, ro * C : (ro + 1) * C] = total.astype(jnp.bfloat16)
        upsample(h_ref, u_ref, slot_ref, spread_ref, b_ref, buf_ref, out_ref, sem, (0, 1, 2, 3), flipped())


def even_first_kernel(
    s_ref, u_ref, slot_ref, spread_ref, first_ref, _, out_ref, h_ref, kept_ref, b_ref, buf_ref, sem
):
    mine, edge = place(0)

    def lower():
        for f in range(2):
            for ro in (2, 3):
                h_ref[f, ro * C : (ro + 1) * C] = hidden_row(s_ref, f, ro, first_ref).astype(jnp.bfloat16)

    @pl.when(jnp.logical_and(mine, edge))
    def _():
        lower()
        for f in range(2):
            h_ref[f, :C] = jnp.zeros((C, 2 * W), jnp.bfloat16)
            h_ref[f, C : 2 * C] = hidden_row(s_ref, f, 1, None).astype(jnp.bfloat16)
        upsample(h_ref, u_ref, slot_ref, spread_ref, b_ref, buf_ref, out_ref, sem, (0, 1, 2, 3), flipped())

    @pl.when(jnp.logical_and(mine, jnp.logical_not(edge)))
    def _():
        lower()
        upsample(h_ref, u_ref, slot_ref, spread_ref, b_ref, kept_ref, None, sem, (3,), flipped())


def even_second_kernel(
    s_ref, u_ref, slot_ref, spread_ref, _, second_ref, low_ref, kept_ref, __, out_ref, h_ref, b_ref, buf_ref, sem, kept_sem
):
    mine, edge = place(0)

    @pl.when(jnp.logical_and(mine, jnp.logical_not(edge)))
    def _():
        kept = [out_copy(kept_ref, out_ref, kept_sem, f, t, (3,), flipped()) for f in range(2) for t in range(2)]
        for copy in kept:
            copy.start()
        for f in range(2):
            for ro in range(2):
                h_ref[f, ro * C : (ro + 1) * C] = hidden_row(s_ref, f, ro, second_ref).astype(jnp.bfloat16)
            h_ref[f, 2 * C : 3 * C] = low_ref[f, 2 * C : 3 * C]
        upsample(h_ref, u_ref, slot_ref, spread_ref, b_ref, buf_ref, out_ref, sem, (0, 1, 2), flipped())
        for copy in kept:
            copy.wait()


VMEM = pl.BlockSpec(memory_space=pltpu.VMEM)
ANY = pl.BlockSpec(memory_space=pl.ANY)


def call(kernel, out_shape, in_specs, flops, out_spec=VMEM, **more):
    out_specs = out_spec if isinstance(out_spec, tuple) else jax.tree.map(lambda _: out_spec, out_shape)
    return pl.pallas_call(
        kernel,
        out_shape=out_shape,
        in_specs=in_specs,
        out_specs=out_specs,
        compiler_params=pltpu.CompilerParams(vmem_limit_bytes=VMEM_LIMIT),
        cost_estimate=pl.CostEstimate(flops=flops, bytes_accessed=4_000_000, transcendentals=0),
        **more,
    )


def swap(value, partner):
    n_dp, n_tm, n_rows = (lax.axis_size(a) for a in AXES)

    def index(d, t, r):
        return (d * n_tm + t) * n_rows + r

    places = [(d, t, r) for d in range(n_dp) for t in range(n_tm) for r in range(n_rows)]
    return lax.ppermute(value, AXES, [(index(*p), index(*partner(*p))) for p in places])


def on_device(latents, slot_tile, norm_gain, conv_weight, up_weight):
    own_tiles, frames, rows = latents.shape[:3]
    n_dp, n_tm, n_rows = (lax.axis_size(a) for a in AXES)
    slots = slot_tile.reshape(1, -1)
    gain = norm_gain.reshape(1, C)
    w = conv_weight.reshape(9, 3 * C, C)
    uw = up_weight.reshape(3, 3 * C2, C)

    def idle(phase):
        return lambda d: (d ^ 1) if phase == 0 else ((d + 1) % n_dp if d % 2 else (d - 1) % n_dp)

    def across_chips(d, t, r):
        if t in (0, n_tm - 1):
            return idle(0)(d), t, r
        return d, (t + 1 if t % 2 else t - 1), r

    def rows_swap(phase, core):
        def partner(d, t, r):
            if t % 2 != core:
                return idle(1 - phase)(d), t, r
            if phase == 0:
                return d, t, r ^ 1
            return d, t, ((r + 1) % n_rows if r % 2 else (r - 1) % n_rows)

        return partner

    def shape(*dims, dtype=jnp.bfloat16):
        return jax.ShapeDtypeStruct(dims, dtype)

    part = jax.ShapeDtypeStruct((2, 4, C, 2 * W), jnp.float32)
    half = jax.ShapeDtypeStruct((2, 2, C, 2 * W), jnp.bfloat16)

    from_chip = swap(latents, lambda d, t, r: (d, t ^ 1, r))
    from_z = swap(latents, across_chips)
    square = jax.ShapeDtypeStruct((2 * W, 2 * W), jnp.bfloat16)
    spread = call(spread_kernel, square, [], 1_500_000_000)()
    s1, spread = call(own_kernel, (part, square), [VMEM] * 4, 1_020_000_000, input_output_aliases={3: 1})(
        latents, gain, w, spread
    )
    specs = [VMEM] * 5
    wide = jax.ShapeDtypeStruct((2, 3 * C2, 2 * C), jnp.bfloat16)
    s, odd1, odd2, u, four = call(
        functools.partial(previous_kernel, 1), (part, half, half, wide, shape(2, 3 * C, 4 * C)), specs, 1_020_000_000
    )(from_chip, gain, w, s1, uw)
    odd1 = swap(odd1, rows_swap(0, 1))
    odd2 = swap(odd2, rows_swap(1, 1))
    s, even1, even2, u = call(
        functools.partial(previous_kernel, 0),
        (part, half, half, wide),
        specs + [VMEM] * 3,
        1_020_000_000,
        input_output_aliases={6: 0, 7: 3},
    )(from_z, gain, w, s1, uw, four, s, u)
    even1 = swap(even1, rows_swap(0, 0))
    even2 = swap(even2, rows_swap(1, 0))
    out = jax.ShapeDtypeStruct((own_tiles, frames, 2 * rows, C2, 2 * W), jnp.bfloat16)
    rows_of = shape(2, 4 * C, 2 * W)
    scratch = [
        pltpu.VMEM((2, 8 * C2, 2 * W), jnp.bfloat16),
        pltpu.VMEM((2, 2, 2 * rows, C2, 2 * W), jnp.bfloat16),
        pltpu.SemaphoreType.DMA((2, 2)),
    ]
    ahead = pltpu.VMEM(rows_of.shape, rows_of.dtype)
    common = (s, u, slots, spread)
    pixels = call(odd_kernel, out, [VMEM] * 6, 9_000_000_000, ANY, scratch_shapes=[ahead] + scratch)(
        *common, odd1, odd2
    )
    pixels, lower, kept = call(
        even_first_kernel,
        (out, rows_of, shape(2, 2, 1, C2, 2 * W)),
        [VMEM] * 5 + [ANY],
        900_000_000,
        (ANY, VMEM, VMEM),
        scratch_shapes=scratch,
        input_output_aliases={5: 0},
    )(*common, even1, pixels)
    return call(
        even_second_kernel,
        out,
        [VMEM] * 8 + [ANY],
        700_000_000,
        ANY,
        scratch_shapes=[ahead] + scratch + [pltpu.SemaphoreType.DMA((2, 2))],
        input_output_aliases={8: 0},
    )(*common, even1, even2, lower, kept, pixels)


def solution(mesh):
    placed = (P("dp", "tm", "rows", None, None), P(), P(), P(), P())
    return jax.shard_map(
        on_device,
        mesh=mesh,
        in_specs=placed,
        out_specs=P("dp", "tm", "rows", None, None),
        check_vma=False,
    )
```

```python
import functools

import jax
import jax.numpy as jnp
from jax import lax
from jax.experimental import pallas as pl
from jax.experimental.pallas import tpu as pltpu
from jax.sharding import PartitionSpec as P

C = 192
C2 = 96
W = 128
VMEM_LIMIT = 16 * 1024 * 1024
AXES = ("dp", "tm", "rows")


def activate(x, gain):
    meansq = jnp.mean(x * x, axis=0, keepdims=True)
    g = x * lax.rsqrt(meansq + 1e-06) * gain
    return (g * jax.nn.sigmoid(g)).astype(jnp.bfloat16)


def column(row):
    i = lax.broadcasted_iota(jnp.int32, (C, C), 0)
    j = lax.broadcasted_iota(jnp.int32, (C, C), 1)
    return jnp.sum(jnp.where(i == j, row, 0.0), axis=1, keepdims=True)


def pair(ref, frame, row):
    return jnp.concatenate([ref[0, frame, row], ref[1, frame, row]], axis=1)


def shifted(p, by):
    lane = lax.broadcasted_iota(jnp.int32, (p.shape[0], W), 1)
    edge = 0 if by == 1 else W - 1
    halves = []
    for t in range(2):
        moved = pltpu.roll(p[:, t * W : (t + 1) * W], by % W, 1)
        halves.append(jnp.where(lane == edge, 0.0, moved))
    return jnp.concatenate(halves, axis=1)


def conv_terms(acts, w_ref, row_out, flip):
    acc = None
    for kt, panels in acts:
        for row in range(2):
            kh = row - row_out + 2
            if 0 <= kh <= 2:
                tap = kt * 3 + jnp.where(flip, 2 - kh, kh)
                term = jnp.dot(w_ref[tap], panels[row], preferred_element_type=jnp.float32)
                acc = term if acc is None else acc + term
    return columns(acc)


def columns(acc):
    return shifted(acc[:C], 1) + acc[C : 2 * C] + shifted(acc[2 * C :], -1)


def flipped():
    return lax.rem(lax.axis_index("rows"), 2) == 1


def panels(x_ref, flip):
    rows = [jnp.where(flip, 1 - r, r) for r in range(2)]
    return [[pair(x_ref, f, r).astype(jnp.float32) for r in rows] for f in range(2)]


def spread_kernel(spread_ref):
    src = lax.broadcasted_iota(jnp.int32, (2 * W, 2 * W), 0)
    dst = lax.broadcasted_iota(jnp.int32, (2 * W, 2 * W), 1)
    spread_ref[...] = (dst == jnp.where(src < W, 2 * src, 2 * (src - W) + 1)).astype(jnp.bfloat16)


def own_kernel(x_ref, gain_ref, w_ref, spread_ref, s_ref, _):
    flip = flipped()
    gain = column(gain_ref[...])
    xs = panels(x_ref, flip)
    a = [[activate(xs[f][r], gain) for r in range(2)] for f in range(2)]
    for fo in range(2):
        for ro in range(4):
            total = conv_terms([(2 - (fo - fi), a[fi]) for fi in range(fo + 1)], w_ref, ro, flip)
            if ro in (1, 2):
                total = total + xs[fo][ro - 1]
            s_ref[fo, ro] = total


def previous_kernel(core, x_ref, gain_ref, w_ref, s1_ref, uw_ref, *refs):
    s_ref, first_ref, second_ref, u_ref = refs[-4:] if core == 0 else refs[:4]
    four_ref = refs[0] if core == 0 else refs[4]
    tm = lax.axis_index("tm")
    flip = flipped()

    @pl.when(lax.rem(tm, 2) == core)
    def _():
        gain = jnp.where(tm > 0, column(gain_ref[...]), 0.0)
        a = [[activate(x, gain) for x in xs] for xs in panels(x_ref, flip)]
        for fo in range(2):
            acts = [(0, a[0]), (1, a[1])] if fo == 0 else [(0, a[1])]
            for ro in range(4):
                if core == 0 and fo == 0 and ro in (1, 2):
                    four = jnp.concatenate(a[0] + a[1], axis=0)
                    terms = columns(jnp.dot(four_ref[ro - 1], four, preferred_element_type=jnp.float32))
                else:
                    terms = conv_terms(acts, w_ref, ro, flip)
                total = s1_ref[fo, ro] + terms
                s_ref[fo, ro] = total
                to_ref = first_ref if ro >= 2 else second_ref
                to_ref[fo, ro % 2] = total.astype(jnp.bfloat16)

    @pl.when(lax.rem(tm, 2) != core)
    def _():
        w0, w1, w2 = (uw_ref[jnp.where(flip, 2 - kh, kh)].astype(jnp.float32) for kh in range(3))
        u_ref[0] = jnp.concatenate([w0, w1 + w2], axis=1).astype(jnp.bfloat16)
        u_ref[1] = jnp.concatenate([w0 + w1, w2], axis=1).astype(jnp.bfloat16)
        if core == 1:
            for ro in (1, 2):
                khs = [row - ro + 2 for row in range(2)]
                taps = [w_ref[kt * 3 + jnp.where(flip, 2 - kh, kh)] for kt in range(2) for kh in khs]
                four_ref[ro - 1] = jnp.concatenate(taps, axis=1)


def hidden_row(s_ref, f, ro, got_ref):
    total = s_ref[f, ro]
    if got_ref is not None:
        total = total + got_ref[f, 1 - ro % 2].astype(jnp.float32)
    return total


def upsample(h_ref, u_ref, slot_ref, spread_ref, b_ref, buf_ref, out_ref, sem, todo, flip):
    spread = spread_ref[...]
    n = len(todo)
    for f in range(2):
        for i, at_row in enumerate(todo):
            low = (at_row // 2 + at_row % 2) * C
            total = jnp.dot(u_ref[at_row % 2], h_ref[f, low : low + 2 * C], preferred_element_type=jnp.float32)
            k0, k1, k2 = total[:C2], total[C2 : 2 * C2], total[2 * C2 :]
            even = (shifted(k0, 1) + k1 + k2).astype(jnp.bfloat16)
            odd = (k0 + k1 + shifted(k2, -1)).astype(jnp.bfloat16)
            for t in range(2):
                at = (t * n + i) * C2
                b_ref[f, at : at + C2, :W] = even[:, t * W : (t + 1) * W]
                b_ref[f, at : at + C2, W:] = odd[:, t * W : (t + 1) * W]
    copies = []
    for f in range(2):
        for t in range(2):
            hit = slot_ref[...] == lax.axis_index("dp") * 2 + t
            keep = jnp.max(jnp.where(hit, 1.0, 0.0), axis=1, keepdims=True)
            wide = jnp.dot(b_ref[f, t * n * C2 : (t + 1) * n * C2], spread, preferred_element_type=jnp.float32)
            wide = (wide * keep).astype(jnp.bfloat16)
            for i in range(n):
                buf_ref[f, t, jnp.where(flip, n - 1 - i, i)] = wide[i * C2 : (i + 1) * C2]
        if out_ref is not None:
            for t in range(2):
                copies.append(out_copy(buf_ref, out_ref, sem, f, t, todo, flip))
                copies[-1].start()
    for copy in copies:
        copy.wait()


def out_copy(buf_ref, out_ref, sem, f, t, todo, flip):
    first, n = jnp.where(flip, 3 - todo[-1], todo[0]), len(todo)
    return pltpu.make_async_copy(buf_ref.at[f, t, pl.ds(0, n)], out_ref.at[t, f, pl.ds(first, n)], sem.at[f, t])


def place(core):
    row = lax.axis_index("rows")
    mine = lax.rem(lax.axis_index("tm"), 2) == core
    return mine, jnp.logical_or(row == 0, row == lax.axis_size("rows") - 1)


def odd_kernel(s_ref, u_ref, slot_ref, spread_ref, first_ref, second_ref, out_ref, h_ref, b_ref, buf_ref, sem):
    mine, edge = place(1)

    @pl.when(mine)
    def _():
        for f in range(2):
            for ro in range(4):
                total = hidden_row(s_ref, f, ro, first_ref if ro >= 2 else second_ref)
                if ro < 2:
                    alone = s_ref[f, ro] if ro == 1 else jnp.zeros_like(total)
                    total = jnp.where(edge, alone, total)
                h_ref[f, ro * C : (ro + 1) * C] = total.astype(jnp.bfloat16)
        upsample(h_ref, u_ref, slot_ref, spread_ref, b_ref, buf_ref, out_ref, sem, (0, 1, 2, 3), flipped())


def even_first_kernel(
    s_ref, u_ref, slot_ref, spread_ref, first_ref, _, out_ref, h_ref, kept_ref, b_ref, buf_ref, sem
):
    mine, edge = place(0)

    def lower():
        for f in range(2):
            for ro in (2, 3):
                h_ref[f, ro * C : (ro + 1) * C] = hidden_row(s_ref, f, ro, first_ref).astype(jnp.bfloat16)

    @pl.when(jnp.logical_and(mine, edge))
    def _():
        lower()
        for f in range(2):
            h_ref[f, :C] = jnp.zeros((C, 2 * W), jnp.bfloat16)
            h_ref[f, C : 2 * C] = hidden_row(s_ref, f, 1, None).astype(jnp.bfloat16)
        upsample(h_ref, u_ref, slot_ref, spread_ref, b_ref, buf_ref, out_ref, sem, (0, 1, 2, 3), flipped())

    @pl.when(jnp.logical_and(mine, jnp.logical_not(edge)))
    def _():
        lower()
        upsample(h_ref, u_ref, slot_ref, spread_ref, b_ref, kept_ref, None, sem, (3,), flipped())


def even_second_kernel(
    s_ref, u_ref, slot_ref, spread_ref, _, second_ref, low_ref, kept_ref, __, out_ref, h_ref, b_ref, buf_ref, sem, kept_sem
):
    mine, edge = place(0)

    @pl.when(jnp.logical_and(mine, jnp.logical_not(edge)))
    def _():
        kept = [out_copy(kept_ref, out_ref, kept_sem, f, t, (3,), flipped()) for f in range(2) for t in range(2)]
        for copy in kept:
            copy.start()
        for f in range(2):
            for ro in range(2):
                h_ref[f, ro * C : (ro + 1) * C] = hidden_row(s_ref, f, ro, second_ref).astype(jnp.bfloat16)
            h_ref[f, 2 * C : 3 * C] = low_ref[f, 2 * C : 3 * C]
        upsample(h_ref, u_ref, slot_ref, spread_ref, b_ref, buf_ref, out_ref, sem, (0, 1, 2), flipped())
        for copy in kept:
            copy.wait()


VMEM = pl.BlockSpec(memory_space=pltpu.VMEM)
ANY = pl.BlockSpec(memory_space=pl.ANY)


def call(kernel, out_shape, in_specs, flops, out_spec=VMEM, **more):
    out_specs = out_spec if isinstance(out_spec, tuple) else jax.tree.map(lambda _: out_spec, out_shape)
    return pl.pallas_call(
        kernel,
        out_shape=out_shape,
        in_specs=in_specs,
        out_specs=out_specs,
        compiler_params=pltpu.CompilerParams(vmem_limit_bytes=VMEM_LIMIT),
        cost_estimate=pl.CostEstimate(flops=flops, bytes_accessed=4_000_000, transcendentals=0),
        **more,
    )


def swap(value, partner):
    n_dp, n_tm, n_rows = (lax.axis_size(a) for a in AXES)

    def index(d, t, r):
        return (d * n_tm + t) * n_rows + r

    places = [(d, t, r) for d in range(n_dp) for t in range(n_tm) for r in range(n_rows)]
    return lax.ppermute(value, AXES, [(index(*p), index(*partner(*p))) for p in places])


def on_device(latents, slot_tile, norm_gain, conv_weight, up_weight):
    own_tiles, frames, rows = latents.shape[:3]
    n_dp, n_tm, n_rows = (lax.axis_size(a) for a in AXES)
    slots = slot_tile.reshape(1, -1)
    gain = norm_gain.reshape(1, C)
    w = conv_weight.reshape(9, 3 * C, C)
    uw = up_weight.reshape(3, 3 * C2, C)

    def idle(phase):
        return lambda d: (d ^ 1) if phase == 0 else ((d + 1) % n_dp if d % 2 else (d - 1) % n_dp)

    def across_chips(d, t, r):
        if t in (0, n_tm - 1):
            return idle(0)(d), t, r
        return d, (t + 1 if t % 2 else t - 1), r

    def rows_swap(phase, core):
        def partner(d, t, r):
            if t % 2 != core:
                return idle(1 - phase if core else phase)(d), t, r
            if phase == 0:
                return d, t, r ^ 1
            return d, t, ((r + 1) % n_rows if r % 2 else (r - 1) % n_rows)

        return partner

    def shape(*dims, dtype=jnp.bfloat16):
        return jax.ShapeDtypeStruct(dims, dtype)

    part = jax.ShapeDtypeStruct((2, 4, C, 2 * W), jnp.float32)
    half = jax.ShapeDtypeStruct((2, 2, C, 2 * W), jnp.bfloat16)

    from_chip = swap(latents, lambda d, t, r: (d, t ^ 1, r))
    from_z = swap(latents, across_chips)
    square = jax.ShapeDtypeStruct((2 * W, 2 * W), jnp.bfloat16)
    spread = call(spread_kernel, square, [], 1_500_000_000)()
    s1, spread = call(own_kernel, (part, square), [VMEM] * 4, 1_020_000_000, input_output_aliases={3: 1})(
        latents, gain, w, spread
    )
    specs = [VMEM] * 5
    wide = jax.ShapeDtypeStruct((2, 3 * C2, 2 * C), jnp.bfloat16)
    s, odd1, odd2, u, four = call(
        functools.partial(previous_kernel, 1), (part, half, half, wide, shape(2, 3 * C, 4 * C)), specs, 1_020_000_000
    )(from_chip, gain, w, s1, uw)
    odd1 = swap(odd1, rows_swap(0, 1))
    odd2 = swap(odd2, rows_swap(1, 1))
    s, even1, even2, u = call(
        functools.partial(previous_kernel, 0),
        (part, half, half, wide),
        specs + [VMEM] * 3,
        1_020_000_000,
        input_output_aliases={6: 0, 7: 3},
    )(from_z, gain, w, s1, uw, four, s, u)
    even1 = swap(even1, rows_swap(0, 0))
    even2 = swap(even2, rows_swap(1, 0))
    out = jax.ShapeDtypeStruct((own_tiles, frames, 2 * rows, C2, 2 * W), jnp.bfloat16)
    rows_of = shape(2, 4 * C, 2 * W)
    scratch = [
        pltpu.VMEM((2, 8 * C2, 2 * W), jnp.bfloat16),
        pltpu.VMEM((2, 2, 2 * rows, C2, 2 * W), jnp.bfloat16),
        pltpu.SemaphoreType.DMA((2, 2)),
    ]
    ahead = pltpu.VMEM(rows_of.shape, rows_of.dtype)
    common = (s, u, slots, spread)
    pixels = call(odd_kernel, out, [VMEM] * 6, 9_000_000_000, ANY, scratch_shapes=[ahead] + scratch)(
        *common, odd1, odd2
    )
    pixels, lower, kept = call(
        even_first_kernel,
        (out, rows_of, shape(2, 2, 1, C2, 2 * W)),
        [VMEM] * 5 + [ANY],
        900_000_000,
        (ANY, VMEM, VMEM),
        scratch_shapes=scratch,
        input_output_aliases={5: 0},
    )(*common, even1, pixels)
    return call(
        even_second_kernel,
        out,
        [VMEM] * 8 + [ANY],
        700_000_000,
        ANY,
        scratch_shapes=[ahead] + scratch + [pltpu.SemaphoreType.DMA((2, 2))],
        input_output_aliases={8: 0},
    )(*common, even1, even2, lower, kept, pixels)


def solution(mesh):
    placed = (P("dp", "tm", "rows", None, None), P(), P(), P(), P())
    return jax.shard_map(
        on_device,
        mesh=mesh,
        in_specs=placed,
        out_specs=P("dp", "tm", "rows", None, None),
        check_vma=False,
    )
```
